256 devices in a mesh: layout: 16 (over y, x), rep: 16 (over z, core).
Axes of the slice: x: 4, y: 4, z: 8, core: 2. Of those that a mesh axis runs over, the one named last changes fastest.
Arguments:
- amplitudes: bfloat16 [48, 1024, 8192], P('rep', 'layout'), may hold values from -6 to 6
- integrals: bfloat16 [48, 1024, 2048], P('rep', None, 'layout'), may hold values from -0.0390625 to 0.0390625
- amp_mask: int32 [4, 8], replicated, may hold values 0 or 1
- int_mask: int32 [8, 4], replicated, may hold values 0 or 1
- occ_row: float32 [16], replicated, may hold values from -1.5 to -0.2
- occ_col: float32 [4], replicated, may hold values from -1.5 to -0.2
- vir_energy: float32 [4, 128], replicated, may hold values from 0.2 to 2
Outputs:
- update: bfloat16 [8192, 2048], P('layout', 'rep')
The draws below stay inside these ranges and needn't reach their ends.
All inputs are finite; a program needn't handle non-finite values.
Results may differ from the reference program's by a relative error of at most 0.001.
Values may be sent and summed in bfloat16 or wider, within the bound.
No kernel may reach another device: no remote copies, remote signals or barrier semaphores. Data moves between devices by JAX's collectives and lax.ppermute only.
A program may use at most 256 MiB of HBM per device.

```python
import math
import jax
import jax.numpy as jnp
from jax import lax

VB = 128
PB = 4
OCC = 48
CB = 8
IW = 16
JW = 4
ROWS = 8192
COLS = 2048


def plant(array, rng, low, high):
    longest = array.shape.index(max(array.shape))
    spots = []
    for shift in (0, 1):
        where = [jax.random.randint(jax.random.fold_in(rng, axis), (), 0, length) for axis, length in enumerate(array.shape)]
        where[longest] = (where[longest] + shift) % array.shape[longest]
        spots.append(tuple(where))
    return array.at[spots[0]].set(low).at[spots[1]].set(high)


def with_spikes(array, own_key, source, target, shards_of, factor):
    def block_of(dim):
        return (jnp.arange(array.shape[dim]) // (array.shape[dim] // shards_of)).reshape((-1,) + (1,) * (array.ndim - 1 - dim))

    one_side = jax.random.permutation(own_key, shards_of)[block_of(target)]
    other_side = (block_of(target) + shards_of // 2) % shards_of
    return jnp.where((block_of(source) == one_side) | (block_of(source) == other_side), factor * array, array)


def shard_levels(stream_key, dims, cuts, low, top_value):
    gain, own = 1.0, jax.random.fold_in(stream_key, 6)
    for dim, blocks in cuts:
        heights = jnp.exp(jax.random.uniform(jax.random.fold_in(own, dim), (blocks,), jnp.float32, low / len(cuts), top_value / len(cuts)))
        gain = gain * jnp.repeat(heights, dims[dim] // blocks).reshape([-1 if axis == dim else 1 for axis in range(len(dims))])
    return gain


def scatter_about(own_key, shape, width, bound, split=(), dtype=jnp.bfloat16):
    values = width * jax.random.normal(own_key, shape, jnp.float32)
    if split:
        values = values * shard_levels(own_key, shape, split, -0.22, 0.18)
    return jnp.clip(values, -bound, bound).astype(dtype)


def heavy_noise(key, dims, scale, reach, pieces, heavy, kind=jnp.bfloat16):
    result = scale * jax.random.normal(key, dims, jnp.float32)
    if pieces:
        result = result * shard_levels(key, dims, pieces, -0.22, 0.18)
    return jnp.clip(with_spikes(result, jax.random.fold_in(key, 3), *heavy), -reach, reach).astype(kind)


def setup_inputs(seed: int = 0) -> dict:
    streams_of = jax.random.split(jax.random.key(seed), 8)
    return {
        "amplitudes": scatter_about(streams_of[0], (OCC, CB * VB, ROWS), 1.0, 6.0, ((0, 16), (1, 16))),
        "integrals": heavy_noise(streams_of[1], (OCC, CB * VB, COLS), (OCC * CB * VB) ** -0.5, 0.0390625, ((0, 16), (2, 16)), (0, 2, 16, 2.0)),
        "amp_mask": plant((jax.random.randint(streams_of[2], (PB, CB), 0, 3) < 2).astype(jnp.int32), jax.random.fold_in(streams_of[2], 1), 0, 1),
        "int_mask": plant((jax.random.randint(streams_of[3], (CB, PB), 0, 3) < 2).astype(jnp.int32), jax.random.fold_in(streams_of[3], 1), 0, 1),
        "occ_row": jnp.clip(jax.random.uniform(streams_of[4], (IW,), jnp.float32, -1.5, -0.2), -1.5, -0.2),
        "occ_col": jnp.clip(jax.random.uniform(streams_of[5], (JW,), jnp.float32, -1.5, -0.2), -1.5, -0.2),
        "vir_energy": jnp.clip(jnp.exp(jax.random.uniform(streams_of[6], (PB, VB), jnp.float32, math.log(0.2), math.log(2.0))), 0.2, 2.0),
    }


def accumulate(running, operands):
    return running + jnp.dot(operands[0].T, operands[1], preferred_element_type=jnp.float32), None


def reference(amplitudes, integrals, amp_mask, int_mask, occ_row, occ_col, vir_energy):
    row_index = jnp.arange(PB * IW * VB)
    col_index = jnp.arange(PB * JW * VB)
    inner_index = jnp.arange(CB * VB)
    amp_keep = amp_mask[row_index // (IW * VB)][:, inner_index // VB].T.astype(jnp.bfloat16)
    col_keep = int_mask[inner_index // VB][:, col_index // (JW * VB)].astype(jnp.bfloat16)
    amp_kept = amplitudes * amp_keep[None]
    int_kept = integrals * col_keep[None]
    start_sum = jnp.zeros((row_index.shape[0], col_index.shape[0]), jnp.float32)
    cycle_sum, _ = lax.scan(accumulate, start_sum, (amp_kept, int_kept))
    row_energy = vir_energy[row_index // (IW * VB), row_index % VB] - occ_row[(row_index // VB) % IW]
    col_energy = vir_energy[col_index // (JW * VB), col_index % VB] - occ_col[(col_index // VB) % JW]
    denominator = -(row_energy[:, None] + col_energy[None, :])
    return (cycle_sum / denominator).astype(jnp.bfloat16)
```

```python
import jax
import jax.numpy as jnp
from jax import lax
from jax.experimental import pallas as pl
from jax.experimental.pallas import tpu as pltpu
from jax.sharding import Mesh, PartitionSpec as P

AXES = ("y", "x", "z", "core")
NY, NX, NZ, NC = 4, 4, 8, 2
KD = 192
RB = 512
KT = 16 * KD
VMEM = pltpu.MemorySpace.VMEM
SMEM = pltpu.MemorySpace.SMEM


def pairs(to):
    out = []
    for y in range(NY):
        for x in range(NX):
            for z in range(NZ):
                for c in range(NC):
                    ty, tx, tz, tc = to(y, x, z, c)
                    src = ((y * NX + x) * NZ + z) * NC + c
                    dst = ((ty % NY * NX + tx % NX) * NZ + tz % NZ) * NC + tc % NC
                    out.append((src, dst))
    return out


UP = pairs(lambda y, x, z, c: (y + 1, x, z, c))
DOWN = pairs(lambda y, x, z, c: (y - 1, x, z, c))
OVER = pairs(lambda y, x, z, c: (y + 2, x, z, c))
PARTNER = pairs(lambda y, x, z, c: (y, 3 - x, z, c))
CROSS = pairs(lambda y, x, z, c: (y, x ^ 1, z, c))
ACROSS = pairs(lambda y, x, z, c: (y, x + 2, z, c))
SWAP = pairs(lambda y, x, z, c: (y, x, z, 1 - c))


def slab_of(y, x, z):
    turn = (z // 2 == 1) * 3 + (z // 2 == 2) * 1 + (z // 2 == 3) * 2
    return (y + turn) % 4, x ^ (z % 2)


def home(y, x, z, c):
    col_y, col_x = slab_of(y, x, z)
    return y, x if c == 0 else 3 - x, 2 * col_y + col_x // 2, col_x % 2


HOME = pairs(home)


def send(value, where):
    return lax.ppermute(value, AXES, where)


def prepare_kernel(place, amp_mask, int_mask, a, b, own, near, up, down, over, scratch):
    y, x = place[0], place[1]
    block_q = 2 * y + x // 2
    low = jnp.minimum(x, 3 - x)
    for to_y, first, second in (
        (y, own, None),
        (lax.rem(y + 1, 4), up.at[0], up.at[1]),
        (lax.rem(y + 3, 4), down.at[0], down.at[1]),
        (lax.rem(y + 2, 4), over.at[0], over.at[1]),
    ):
        keep = amp_mask[to_y, block_q].astype(jnp.float32).astype(jnp.bfloat16)
        for dst, lo in ((first, low), (second, 1 - low)):
            for half in range(2):
                to_x = lo if half == 0 else 3 - lo
                start = pl.multiple_of((to_y * 4 + to_x) * RB, RB)
                for k in range(3):
                    value = a[k, :, pl.ds(start, RB)] * keep
                    if dst is None:
                        near[pl.ds(128, 64), pl.ds((2 * k + half) * RB, RB)] = value
                    else:
                        dst[pl.ds(k * 64, 64), pl.ds(half * RB, RB)] = value
    for slab in range(16):
        keep = int_mask[slab // 2, y].astype(jnp.float32).astype(jnp.bfloat16)
        at = ((slab % 4) * 4 + slab // 4) * KD
        for k in range(3):
            scratch[pl.ds(at + k * 64, 64), :] = b[k, pl.ds(slab * 64, 64), :] * keep
    for j in range(KT // 128):
        near[pl.ds(0, 128), pl.ds(j * 128, 128)] = scratch[pl.ds(j * 128, 128), :].T


def prepare(place, amp_mask, int_mask, a, b):
    piece = jax.ShapeDtypeStruct((KD, 2 * RB), jnp.bfloat16)
    two = jax.ShapeDtypeStruct((2, KD, 2 * RB), jnp.bfloat16)
    near = jax.ShapeDtypeStruct((KD, KT), jnp.bfloat16)
    smem = pl.BlockSpec(memory_space=SMEM)
    vmem = pl.BlockSpec(memory_space=VMEM)
    return pl.pallas_call(
        prepare_kernel,
        out_shape=(piece, near, two, two, two),
        in_specs=[smem, smem, smem, vmem, vmem],
        out_specs=(vmem,) * 5,
        scratch_shapes=[pltpu.VMEM((KT, 128), jnp.bfloat16)],
        compiler_params=pltpu.CompilerParams(vmem_limit_bytes=24 << 20),
        cost_estimate=pl.CostEstimate(flops=0, bytes_accessed=8 << 20, transcendentals=0),
        name="prepare",
    )(place, amp_mask, int_mask, a, b)


def gather_kernel(near, from_near, down, up, over, early, own_rest, oth_rest, oth_all, b_here):
    del early
    for j, ref in enumerate((down, up, over)):
        own_rest[j] = ref[0]
        oth_rest[j] = ref[1]
        oth_all[j] = ref[1]
    for k in range(3):
        oth_all[3, pl.ds(k * 64, 64), :] = near[pl.ds(128, 64), pl.ds(k * 2 * RB, 2 * RB)]
    b_here[pl.ds(0, 128), :] = near[pl.ds(0, 128), :]
    b_here[pl.ds(128, 128), :] = from_near[...]


def gather(near, from_near, down, up, over, early):
    def shape(n):
        return jax.ShapeDtypeStruct((n, KD, 2 * RB), jnp.bfloat16)

    vmem = pl.BlockSpec(memory_space=VMEM)
    return pl.pallas_call(
        gather_kernel,
        out_shape=(shape(3), shape(3), shape(4), jax.ShapeDtypeStruct((256, KT), jnp.bfloat16)),
        grid=(1,),
        in_specs=[
            vmem,
            pl.BlockSpec((128, KT), lambda i: (0, 0)),
            vmem,
            vmem,
            vmem,
            pl.BlockSpec(memory_space=pl.ANY),
        ],
        out_specs=(vmem,) * 4,
        compiler_params=pltpu.CompilerParams(vmem_limit_bytes=24 << 20),
        cost_estimate=pl.CostEstimate(flops=0, bytes_accessed=10 << 20, transcendentals=0),
        name="gather",
    )(near, from_near, down, up, over, early)


def arrange_kernel(place, half, s0, s1, s2, s3, p0, p1, c0, c1, x1, out):
    y, x = place[0], place[1]

    def put(ref, from_x, from_y):
        at = pl.multiple_of((from_x * 4 + from_y) * KD, KD)
        out[pl.ds(at, KD), :] = ref[...]

    around = (lax.rem(y + 3, 4), lax.rem(y + 1, 4), lax.rem(y + 2, 4))
    put(s0, x, y)
    for ref, from_y in zip((s1, s2, s3), around):
        put(ref.at[0], x, from_y)
    far = lax.rem(x + 2, 4)
    near = x + 1 - 2 * lax.rem(x, 2)
    put(p0, 3 - x, y)
    at = pl.multiple_of((near * 4 + y) * KD, KD)
    for k in range(3):
        start = pl.multiple_of(k * 2 * RB + half[0] * RB + pl.program_id(0) * 256, 256)
        out[pl.ds(at + k * 64, 64), :] = c0[:, pl.ds(start, 256)]
    put(x1.at[3], far, y)
    for late, from_x in ((p1, 3 - x), (c1, near), (x1, far)):
        for j, from_y in enumerate(around):
            put(late.at[j], from_x, from_y)


def arrange(place, half, amps):
    wide = 256

    def lanes(lead=None):
        if lead is None:
            return pl.BlockSpec((KD, wide), lambda i, pr, hr: (0, 2 * hr[0] + i))
        return pl.BlockSpec((lead, KD, wide), lambda i, pr, hr: (0, 0, 2 * hr[0] + i))

    specs = [lanes()] + [lanes(1)] * 3
    specs += [lanes(), lanes(3), pl.BlockSpec((64, KT), lambda i, pr, hr: (2, 0)), lanes(3), lanes(4)]
    return pl.pallas_call(
        arrange_kernel,
        out_shape=jax.ShapeDtypeStruct((KT, RB), jnp.bfloat16),
        grid_spec=pltpu.PrefetchScalarGridSpec(
            num_scalar_prefetch=2,
            grid=(RB // wide,),
            in_specs=specs,
            out_specs=pl.BlockSpec((KT, wide), lambda i, pr, hr: (0, i)),
        ),
        compiler_params=pltpu.CompilerParams(vmem_limit_bytes=24 << 20),
        cost_estimate=pl.CostEstimate(flops=0, bytes_accessed=6 << 20, transcendentals=0),
        name="arrange",
    )(place, half, *amps)


def product(place, half, amps, ints):
    right = arrange(place, half, amps)
    return [jnp.dot(left, right, preferred_element_type=jnp.float32) for left in ints]


def local(amplitudes, integrals, amp_mask, int_mask, occ_row, occ_col, vir_energy):
    y, x, z, core = (lax.axis_index(name) for name in AXES)
    place = jnp.stack([y, x]).astype(jnp.int32)
    own, near, up, down, over = prepare(place, amp_mask, int_mask, amplitudes, integrals)

    from_down = send(up, UP)
    from_up = send(down, DOWN)
    from_over = send(over, OVER)
    from_near = send(near, CROSS)
    p0 = send(own, PARTNER)

    own_rest, oth_rest, oth_all, b_here = gather(
        near, from_near, from_down, from_up, from_over, p0
    )
    b_down = send(b_here, UP)
    b_up = send(b_here, DOWN)
    p1 = send(own_rest, PARTNER)
    c1 = send(oth_rest, CROSS)
    x1 = send(oth_all, ACROSS)
    b_far0 = send(b_down[:128], UP)
    b_far1 = send(b_up[128:], DOWN)

    amps = (own, from_down, from_up, from_over, p0, p1, from_near, c1, x1)
    ints = (b_here, b_down, b_up, b_far0, b_far1)
    keep_half = jnp.bitwise_xor(x // 2, core).astype(jnp.int32)
    given = jnp.concatenate(product(place, (1 - keep_half)[None], amps, ints))
    taken = send(given, SWAP)
    kept = jnp.concatenate(product(place, keep_half[None], amps, ints))
    cycle_sum = lax.psum_scatter(
        (kept + taken).reshape(8, 128, RB), "z", scatter_dimension=0, tiled=True
    )[0]

    row_x = jnp.where(core == 0, x, 3 - x)
    row_occ = lax.dynamic_slice(occ_row, (4 * row_x,), (4,))
    row_vir = lax.dynamic_slice(vir_energy, (y, 0), (1, 128))
    row_energy = (row_vir - row_occ[:, None]).reshape(-1)
    col_y, col_x = slab_of(y, x, z)
    col_occ = lax.dynamic_slice(occ_col, (col_x,), (1,))
    col_energy = lax.dynamic_slice(vir_energy, (col_y, 0), (1, 128))[0] - col_occ
    denominator = -(row_energy[:, None] + col_energy[None, :])
    return send((cycle_sum.T / denominator).astype(jnp.bfloat16), HOME)


def solution(mesh):
    grid = Mesh(mesh.devices.reshape(NY, NX, NZ, NC), AXES)
    layout, rep = ("y", "x"), ("z", "core")
    placed = (P(rep, layout, None), P(rep, None, layout), P(), P(), P(), P(), P())
    return jax.shard_map(
        local, mesh=grid, in_specs=placed, out_specs=P(layout, rep), check_vma=False
    )
```

```python
import jax
import jax.numpy as jnp
from jax import lax
from jax.experimental import pallas as pl
from jax.experimental.pallas import tpu as pltpu
from jax.sharding import Mesh, PartitionSpec as P

AXES = ("y", "x", "z", "core")
NY, NX, NZ, NC = 4, 4, 8, 2
KD = 192
RB = 512
KT = 16 * KD
VMEM = pltpu.MemorySpace.VMEM
SMEM = pltpu.MemorySpace.SMEM


def pairs(to):
    out = []
    for y in range(NY):
        for x in range(NX):
            for z in range(NZ):
                for c in range(NC):
                    ty, tx, tz, tc = to(y, x, z, c)
                    src = ((y * NX + x) * NZ + z) * NC + c
                    dst = ((ty % NY * NX + tx % NX) * NZ + tz % NZ) * NC + tc % NC
                    out.append((src, dst))
    return out


UP = pairs(lambda y, x, z, c: (y + 1, x, z, c))
DOWN = pairs(lambda y, x, z, c: (y - 1, x, z, c))
OVER = pairs(lambda y, x, z, c: (y + 2, x, z, c))
PARTNER = pairs(lambda y, x, z, c: (y, 3 - x, z, c))
CROSS = pairs(lambda y, x, z, c: (y, x ^ 1, z, c))
ACROSS = pairs(lambda y, x, z, c: (y, x + 2, z, c))
SWAP = pairs(lambda y, x, z, c: (y, x, z, 1 - c))


def slab_of(x, z):
    return z // 2, 2 * (x // 2) + z % 2


def home(y, x, z, c):
    col_y, col_x = slab_of(x, z)
    return y, x if c == 0 else 3 - x, 2 * col_y + col_x // 2, col_x % 2


HOME = pairs(home)


def send(value, where):
    return lax.ppermute(value, AXES, where)


def prepare_kernel(place, amp_mask, int_mask, a, b, own, oth, near, up, down, over, scratch):
    y, x = place[0], place[1]
    block_q = 2 * y + x // 2
    low = jnp.minimum(x, 3 - x)
    for to_y, first, second in (
        (y, own, oth),
        (lax.rem(y + 1, 4), up.at[0], up.at[1]),
        (lax.rem(y + 3, 4), down.at[0], down.at[1]),
        (lax.rem(y + 2, 4), over.at[0], over.at[1]),
    ):
        keep = amp_mask[to_y, block_q].astype(jnp.float32).astype(jnp.bfloat16)
        for dst, lo in ((first, low), (second, 1 - low)):
            for half in range(2):
                to_x = lo if half == 0 else 3 - lo
                start = pl.multiple_of((to_y * 4 + to_x) * RB, RB)
                for k in range(3):
                    value = a[k, :, pl.ds(start, RB)] * keep
                    dst[pl.ds(k * 64, 64), pl.ds(half * RB, RB)] = value
                    if dst is oth:
                        near[pl.ds(128, 64), pl.ds((2 * k + half) * RB, RB)] = value
    for slab in range(16):
        keep = int_mask[slab // 2, y].astype(jnp.float32).astype(jnp.bfloat16)
        at = ((slab % 4) * 4 + slab // 4) * KD
        for k in range(3):
            scratch[pl.ds(at + k * 64, 64), :] = b[k, pl.ds(slab * 64, 64), :] * keep
    for j in range(KT // 128):
        near[pl.ds(0, 128), pl.ds(j * 128, 128)] = scratch[pl.ds(j * 128, 128), :].T


def prepare(place, amp_mask, int_mask, a, b):
    piece = jax.ShapeDtypeStruct((KD, 2 * RB), jnp.bfloat16)
    two = jax.ShapeDtypeStruct((2, KD, 2 * RB), jnp.bfloat16)
    near = jax.ShapeDtypeStruct((KD, KT), jnp.bfloat16)
    smem = pl.BlockSpec(memory_space=SMEM)
    vmem = pl.BlockSpec(memory_space=VMEM)
    return pl.pallas_call(
        prepare_kernel,
        out_shape=(piece, piece, near, two, two, two),
        in_specs=[smem, smem, smem, vmem, vmem],
        out_specs=(vmem,) * 6,
        scratch_shapes=[pltpu.VMEM((KT, 128), jnp.bfloat16)],
        compiler_params=pltpu.CompilerParams(vmem_limit_bytes=24 << 20),
        cost_estimate=pl.CostEstimate(flops=0, bytes_accessed=8 << 20, transcendentals=0),
        name="prepare",
    )(place, amp_mask, int_mask, a, b)


def gather_kernel(near, from_near, down, up, over, p0, x0, own_rest, oth_rest, b_here):
    del p0, x0
    for j, ref in enumerate((down, up, over)):
        own_rest[j] = ref[0]
        oth_rest[j] = ref[1]
    b_here[pl.ds(0, 128), :] = near[...]
    b_here[pl.ds(128, 128), :] = from_near[...]


def gather(*parts):
    rest = jax.ShapeDtypeStruct((3, KD, 2 * RB), jnp.bfloat16)
    vmem = pl.BlockSpec(memory_space=VMEM)
    slab = pl.BlockSpec((128, KT), lambda i: (0, 0))
    anywhere = pl.BlockSpec(memory_space=pl.ANY)
    return pl.pallas_call(
        gather_kernel,
        out_shape=(rest, rest, jax.ShapeDtypeStruct((256, KT), jnp.bfloat16)),
        grid=(1,),
        in_specs=[slab, slab, vmem, vmem, vmem, anywhere, anywhere],
        out_specs=(vmem,) * 3,
        compiler_params=pltpu.CompilerParams(vmem_limit_bytes=16 << 20),
        cost_estimate=pl.CostEstimate(flops=0, bytes_accessed=8 << 20, transcendentals=0),
        name="gather",
    )(*parts)


def six_kernel(place, here, down, up, out):
    odd = lax.rem(place[1], 2)
    for which, ref in enumerate((here, down, up)):

        @pl.when(pl.program_id(0) == which)
        def _(ref=ref):
            out[pl.ds(pl.multiple_of(odd * 128, 128), 128), :] = ref[pl.ds(0, 128), :]
            out[pl.ds(pl.multiple_of((1 - odd) * 128, 128), 128), :] = ref[pl.ds(128, 128), :]


def six(place, *parts):
    def spot(i, pr):
        return (lax.rem(pr[0] + jnp.where(i == 0, 0, jnp.where(i == 1, 3, 1)), 4), 0)

    return pl.pallas_call(
        six_kernel,
        out_shape=jax.ShapeDtypeStruct((1024, KT), jnp.bfloat16),
        grid_spec=pltpu.PrefetchScalarGridSpec(
            num_scalar_prefetch=1,
            grid=(3,),
            in_specs=[pl.BlockSpec((256, KT), lambda i, pr: (0, 0))] * 3,
            out_specs=pl.BlockSpec((256, KT), spot),
        ),
        compiler_params=pltpu.CompilerParams(vmem_limit_bytes=16 << 20),
        cost_estimate=pl.CostEstimate(flops=0, bytes_accessed=9 << 20, transcendentals=0),
        name="six",
    )(place, *parts)


def eight_kernel(place, six_ref, far0, far1, out):
    del six_ref
    odd = lax.rem(place[1], 2)
    out[pl.ds(pl.multiple_of(odd * 128, 128), 128), :] = far0[...]
    out[pl.ds(pl.multiple_of((1 - odd) * 128, 128), 128), :] = far1[...]


def eight(place, slabs, far0, far1):
    slab = pl.BlockSpec((128, KT), lambda i, pr: (0, 0))
    return pl.pallas_call(
        eight_kernel,
        out_shape=jax.ShapeDtypeStruct((1024, KT), jnp.bfloat16),
        grid_spec=pltpu.PrefetchScalarGridSpec(
            num_scalar_prefetch=1,
            grid=(1,),
            in_specs=[pl.BlockSpec(memory_space=pl.ANY), slab, slab],
            out_specs=pl.BlockSpec((256, KT), lambda i, pr: (lax.rem(pr[0] + 2, 4), 0)),
        ),
        input_output_aliases={1: 0},
        compiler_params=pltpu.CompilerParams(vmem_limit_bytes=16 << 20),
        cost_estimate=pl.CostEstimate(flops=0, bytes_accessed=3 << 20, transcendentals=0),
        name="eight",
    )(place, slabs, far0, far1)


def arrange_kernel(place, half, s0, s1, s2, s3, p0, p1, c0, c1, x0, x1, out):
    y, x = place[0], place[1]

    def put(ref, from_x, from_y):
        at = pl.multiple_of((from_x * 4 + from_y) * KD, KD)
        out[pl.ds(at, KD), :] = ref[...]

    around = (lax.rem(y + 3, 4), lax.rem(y + 1, 4), lax.rem(y + 2, 4))
    put(s0, x, y)
    for ref, from_y in zip((s1, s2, s3), around):
        put(ref.at[0], x, from_y)
    far = lax.rem(x + 2, 4)
    near = x + 1 - 2 * lax.rem(x, 2)
    put(p0, 3 - x, y)
    at = pl.multiple_of((near * 4 + y) * KD, KD)
    for k in range(3):
        start = pl.multiple_of(k * 2 * RB + half[0] * RB + pl.program_id(0) * 256, 256)
        out[pl.ds(at + k * 64, 64), :] = c0[:, pl.ds(start, 256)]
    put(x0, far, y)
    for late, from_x in ((p1, 3 - x), (c1, near), (x1, far)):
        for j, from_y in enumerate(around):
            put(late.at[j], from_x, from_y)


def arrange(place, half, amps):
    wide = 256

    def lanes(lead=None):
        if lead is None:
            return pl.BlockSpec((KD, wide), lambda i, pr, hr: (0, 2 * hr[0] + i))
        return pl.BlockSpec((lead, KD, wide), lambda i, pr, hr: (0, 0, 2 * hr[0] + i))

    specs = [lanes()] + [lanes(1)] * 3
    specs += [lanes(), lanes(3), pl.BlockSpec((64, KT), lambda i, pr, hr: (2, 0)), lanes(3)]
    specs += [lanes(), lanes(3)]
    return pl.pallas_call(
        arrange_kernel,
        out_shape=jax.ShapeDtypeStruct((KT, RB), jnp.bfloat16),
        grid_spec=pltpu.PrefetchScalarGridSpec(
            num_scalar_prefetch=2,
            grid=(RB // wide,),
            in_specs=specs,
            out_specs=pl.BlockSpec((KT, wide), lambda i, pr, hr: (0, i)),
        ),
        compiler_params=pltpu.CompilerParams(vmem_limit_bytes=24 << 20),
        cost_estimate=pl.CostEstimate(flops=0, bytes_accessed=6 << 20, transcendentals=0),
        name="arrange",
    )(place, half, *amps)


def finish_kernel(total, row, col, out):
    out[...] = (total[...] / -(row[...] + col[...])).T.astype(jnp.bfloat16)


def finish(total, row, col):
    return pl.pallas_call(
        finish_kernel,
        out_shape=jax.ShapeDtypeStruct((RB, 128), jnp.bfloat16),
        in_specs=[pl.BlockSpec(memory_space=VMEM)] * 3,
        out_specs=pl.BlockSpec(memory_space=VMEM),
        compiler_params=pltpu.CompilerParams(vmem_limit_bytes=16 << 20),
        name="finish",
    )(total, row, col)


def local(amplitudes, integrals, amp_mask, int_mask, occ_row, occ_col, vir_energy):
    y, x, z, core = (lax.axis_index(name) for name in AXES)
    place = jnp.stack([y, x]).astype(jnp.int32)
    own, oth, near, up, down, over = prepare(place, amp_mask, int_mask, amplitudes, integrals)

    from_down = send(up, UP)
    from_up = send(down, DOWN)
    from_over = send(over, OVER)
    from_near = send(near, CROSS)
    p0 = send(own, PARTNER)
    x0 = send(oth, ACROSS)

    own_rest, oth_rest, b_here = gather(near, from_near, from_down, from_up, from_over, p0, x0)
    b_down = send(b_here, UP)
    b_up = send(b_here, DOWN)
    p1 = send(own_rest, PARTNER)
    c1 = send(oth_rest, CROSS)
    x1 = send(oth_rest, ACROSS)
    b_far0 = send(b_down[:128], UP)
    b_far1 = send(b_up[128:], DOWN)
    slabs = eight(place, six(place, b_here, b_down, b_up), b_far0, b_far1)

    amps = (own, from_down, from_up, from_over, p0, p1, from_near, c1, x0, x1)
    keep_half = jnp.bitwise_xor(x // 2, core).astype(jnp.int32)
    give = arrange(place, (1 - keep_half)[None], amps)
    given = jnp.dot(slabs, give, preferred_element_type=jnp.float32)
    taken = send(given, SWAP)
    keep = arrange(place, keep_half[None], amps)
    kept = jnp.dot(slabs, keep, preferred_element_type=jnp.float32)
    cycle_sum = lax.psum_scatter(
        (kept + taken).reshape(8, 128, RB), "z", scatter_dimension=0, tiled=True
    )[0]

    row_x = jnp.where(core == 0, x, 3 - x)
    row_occ = lax.dynamic_slice(occ_row, (4 * row_x,), (4,))
    row_vir = lax.dynamic_slice(vir_energy, (y, 0), (1, 128))
    row_energy = (row_vir - row_occ[:, None]).reshape(1, RB)
    col_y, col_x = slab_of(x, z)
    col_occ = lax.dynamic_slice(occ_col, (col_x,), (1,))
    col_energy = (lax.dynamic_slice(vir_energy, (col_y, 0), (1, 128)) - col_occ).reshape(128, 1)
    return send(finish(cycle_sum, row_energy, col_energy), HOME)


def solution(mesh):
    grid = Mesh(mesh.devices.reshape(NY, NX, NZ, NC), AXES)
    layout, rep = ("y", "x"), ("z", "core")
    placed = (P(rep, layout, None), P(rep, None, layout), P(), P(), P(), P(), P())
    return jax.shard_map(
        local, mesh=grid, in_specs=placed, out_specs=P(layout, rep), check_vma=False
    )
```

```python
import jax
import jax.numpy as jnp
from jax import lax
from jax.experimental import pallas as pl
from jax.experimental.pallas import tpu as pltpu
from jax.sharding import Mesh, PartitionSpec as P

AXES = ("y", "x", "z", "core")
NY, NX, NZ, NC = 4, 4, 8, 2
KD = 192
RB = 512
KT = 16 * KD
VMEM = pltpu.MemorySpace.VMEM


def pairs(to):
    out = []
    for y in range(NY):
        for x in range(NX):
            for z in range(NZ):
                for c in range(NC):
                    ty, tx, tz, tc = to(y, x, z, c)
                    src = ((y * NX + x) * NZ + z) * NC + c
                    dst = ((ty % NY * NX + tx % NX) * NZ + tz % NZ) * NC + tc % NC
                    out.append((src, dst))
    return out


UP = pairs(lambda y, x, z, c: (y + 1, x, z, c))
DOWN = pairs(lambda y, x, z, c: (y - 1, x, z, c))
OVER = pairs(lambda y, x, z, c: (y + 2, x, z, c))
PARTNER = pairs(lambda y, x, z, c: (y, 3 - x, z, c))
CROSS = pairs(lambda y, x, z, c: (y, x ^ 1, z, c))
ACROSS = pairs(lambda y, x, z, c: (y, x + 2, z, c))
AHEAD = pairs(lambda y, x, z, c: (y, x, z + 1, c))
BEHIND = pairs(lambda y, x, z, c: (y, x, z - 1, c))
SWAP = pairs(lambda y, x, z, c: (y, x, z, 1 - c))


def slab_of(x, z):
    return z // 2, 2 * (x // 2) + z % 2


def home(y, x, z, c):
    col_y, col_x = slab_of(x, z)
    return y, x if c == 0 else 3 - x, 2 * col_y + col_x // 2, col_x % 2


HOME = pairs(home)


def send(value, where):
    return lax.ppermute(value, AXES, where)


def prepare_kernel(
    place, amp_mask, int_mask, a_any, b_any, own, oth, near, up, down, over, a, b, scratch, sems
):
    y, x = place[0], place[1]
    block_q = 2 * y + x // 2
    low = jnp.minimum(x, 3 - x)
    turns = (y, lax.rem(y + 1, 4), lax.rem(y + 3, 4), lax.rem(y + 2, 4))
    moves = [pltpu.make_async_copy(b_any, b, sems.at[4])]
    for j, to_y in enumerate(turns):
        lanes = pl.ds(pl.multiple_of(to_y * 4 * RB, 4 * RB), 4 * RB)
        moves.append(pltpu.make_async_copy(a_any.at[:, :, lanes], a.at[j], sems.at[j]))
    for move in moves:
        move.start()
    moves[0].wait()
    for slab in range(16):
        keep = int_mask[y, slab // 2].astype(jnp.float32).astype(jnp.bfloat16)
        at = ((slab % 4) * 4 + slab // 4) * KD
        for k in range(3):
            scratch[pl.ds(at + k * 64, 64), :] = b[k, pl.ds(slab * 64, 64), :] * keep
    for j in range(KT // 128):
        near[pl.ds(0, 128), pl.ds(j * 128, 128)] = scratch[pl.ds(j * 128, 128), :].T
    for j, (first, second) in enumerate(
        ((own, oth), (up.at[0], up.at[1]), (down.at[0], down.at[1]), (over.at[0], over.at[1]))
    ):
        moves[1 + j].wait()
        keep = amp_mask[turns[j], block_q].astype(jnp.float32).astype(jnp.bfloat16)
        for dst, lo in ((first, low), (second, 1 - low)):
            for half in range(2):
                to_x = lo if half == 0 else 3 - lo
                start = pl.multiple_of(to_x * RB, RB)
                for k in range(3):
                    value = a[j, k, :, pl.ds(start, RB)] * keep
                    dst[pl.ds(k * 64, 64), pl.ds(half * RB, RB)] = value
                    if dst is oth:
                        near[pl.ds(128, 64), pl.ds((2 * k + half) * RB, RB)] = value


def prepare(place, amp_mask, int_mask, a, b):
    piece = jax.ShapeDtypeStruct((KD, 2 * RB), jnp.bfloat16)
    two = jax.ShapeDtypeStruct((2, KD, 2 * RB), jnp.bfloat16)
    near = jax.ShapeDtypeStruct((KD, KT), jnp.bfloat16)
    anywhere = pl.BlockSpec(memory_space=pl.ANY)
    vmem = pl.BlockSpec(memory_space=VMEM)
    return pl.pallas_call(
        prepare_kernel,
        out_shape=(piece, piece, near, two, two, two),
        grid_spec=pltpu.PrefetchScalarGridSpec(
            num_scalar_prefetch=3,
            grid=(1,),
            in_specs=[anywhere, anywhere],
            out_specs=(vmem,) * 6,
            scratch_shapes=[
                pltpu.VMEM((4, 3, 64, 4 * RB), jnp.bfloat16),
                pltpu.VMEM((3, 1024, 128), jnp.bfloat16),
                pltpu.VMEM((KT, 128), jnp.bfloat16),
                pltpu.SemaphoreType.DMA((5,)),
            ],
        ),
        compiler_params=pltpu.CompilerParams(vmem_limit_bytes=58 << 20),
        cost_estimate=pl.CostEstimate(flops=0, bytes_accessed=8 << 20, transcendentals=0),
        name="prepare",
    )(place, amp_mask, int_mask.T, a, b)


def follow_kernel(value, after, out):
    del after
    out[...] = value[...]


def follow(value, after):
    vmem = pl.BlockSpec(memory_space=VMEM)
    return pl.pallas_call(
        follow_kernel,
        out_shape=jax.ShapeDtypeStruct(value.shape, value.dtype),
        in_specs=[vmem, pl.BlockSpec(memory_space=pl.ANY)],
        out_specs=vmem,
        compiler_params=pltpu.CompilerParams(vmem_limit_bytes=4 << 20),
        cost_estimate=pl.CostEstimate(flops=0, bytes_accessed=1 << 20, transcendentals=0),
        name="follow",
    )(value, after)


def gather_kernel(near, from_near, down, up, over, p0, x0, own_rest, oth_rest, b_here):
    del p0, x0
    for j, ref in enumerate((down, up, over)):
        own_rest[j] = ref[0]
        oth_rest[j] = ref[1]
    b_here[pl.ds(0, 128), :] = near[...]
    b_here[pl.ds(128, 128), :] = from_near[...]


def gather(*parts):
    rest = jax.ShapeDtypeStruct((3, KD, 2 * RB), jnp.bfloat16)
    vmem = pl.BlockSpec(memory_space=VMEM)
    slab = pl.BlockSpec((128, KT), lambda i: (0, 0))
    anywhere = pl.BlockSpec(memory_space=pl.ANY)
    return pl.pallas_call(
        gather_kernel,
        out_shape=(rest, rest, jax.ShapeDtypeStruct((256, KT), jnp.bfloat16)),
        grid=(1,),
        in_specs=[slab, slab, vmem, vmem, vmem, anywhere, anywhere],
        out_specs=(vmem,) * 3,
        compiler_params=pltpu.CompilerParams(vmem_limit_bytes=16 << 20),
        cost_estimate=pl.CostEstimate(flops=0, bytes_accessed=8 << 20, transcendentals=0),
        name="gather",
    )(*parts)


def run(moves, sems):
    copies = [pltpu.make_async_copy(src, dst, sems.at[i]) for i, (src, dst) in enumerate(moves)]
    for copy in copies:
        copy.start()
    for copy in copies:
        copy.wait()


def join_kernel(place, here, down, up, far0, far1, out, sems):
    y, odd, z = place[0], lax.rem(place[1], 2), place[2]
    moves = []
    for turn, first, second in ((0, here, here), (3, down, down), (1, up, up), (2, far0, far1)):
        at = lax.rem(y + turn, 4) * 2
        skip = 0 if first is far0 else 128
        for bit, src in ((odd, first.at[pl.ds(0, 128), :]), (1 - odd, second.at[pl.ds(skip, 128), :])):
            ahead = lax.rem(at + bit - z + 8, 8)
            spot = jnp.where(ahead == 0, 7, jnp.where(ahead < 5, 7 - 2 * ahead, 2 * ahead - 8))
            spot = jnp.maximum(spot, 0)
            moves.append((src, out.at[pl.ds(pl.multiple_of(spot * 128, 128), 128), :]))
    run(moves, sems)


def join(place, *parts):
    return pl.pallas_call(
        join_kernel,
        out_shape=jax.ShapeDtypeStruct((1024, KT), jnp.bfloat16),
        grid_spec=pltpu.PrefetchScalarGridSpec(
            num_scalar_prefetch=1,
            grid=(1,),
            in_specs=[pl.BlockSpec(memory_space=pl.ANY)] * 5,
            out_specs=pl.BlockSpec(memory_space=VMEM),
            scratch_shapes=[pltpu.SemaphoreType.DMA((8,))],
        ),
        compiler_params=pltpu.CompilerParams(vmem_limit_bytes=16 << 20),
        cost_estimate=pl.CostEstimate(flops=0, bytes_accessed=6 << 20, transcendentals=0),
        name="join",
    )(place, *parts)


def arrange_kernel(place, half, s0, s1, s2, s3, p0, p1, c0, c1, x0, x1, out, sems):
    y, x = place[0], place[1]
    first = pl.multiple_of(half[0] * RB, RB)
    lanes = pl.ds(first, RB)
    moves = []

    def put(ref, from_x, from_y):
        at = pl.multiple_of((from_x * 4 + from_y) * KD, KD)
        moves.append((ref.at[:, lanes], out.at[pl.ds(at, KD), :]))

    around = (lax.rem(y + 3, 4), lax.rem(y + 1, 4), lax.rem(y + 2, 4))
    put(s0, x, y)
    for ref, from_y in zip((s1, s2, s3), around):
        put(ref.at[0], x, from_y)
    far = lax.rem(x + 2, 4)
    near = x + 1 - 2 * lax.rem(x, 2)
    put(p0, 3 - x, y)
    at = pl.multiple_of((near * 4 + y) * KD, KD)
    for k in range(3):
        source = pl.ds(pl.multiple_of(k * 2 * RB + first, RB), RB)
        moves.append((c0.at[pl.ds(128, 64), source], out.at[pl.ds(at + k * 64, 64), :]))
    put(x0, far, y)
    for late, from_x in ((p1, 3 - x), (c1, near), (x1, far)):
        for j, from_y in enumerate(around):
            put(late.at[j], from_x, from_y)
    run(moves, sems)


def arrange(place, half, amps):
    return pl.pallas_call(
        arrange_kernel,
        out_shape=jax.ShapeDtypeStruct((KT, RB), jnp.bfloat16),
        grid_spec=pltpu.PrefetchScalarGridSpec(
            num_scalar_prefetch=2,
            grid=(1,),
            in_specs=[pl.BlockSpec(memory_space=pl.ANY)] * 10,
            out_specs=pl.BlockSpec(memory_space=VMEM),
            scratch_shapes=[pltpu.SemaphoreType.DMA((18,))],
        ),
        compiler_params=pltpu.CompilerParams(vmem_limit_bytes=16 << 20),
        cost_estimate=pl.CostEstimate(flops=0, bytes_accessed=6 << 20, transcendentals=0),
        name="arrange",
    )(place, half, *amps)


def finish_kernel(total, row, col, out):
    out[...] = (total[...] / -(row[...] + col[...])).T.astype(jnp.bfloat16)


def finish(total, row, col):
    return pl.pallas_call(
        finish_kernel,
        out_shape=jax.ShapeDtypeStruct((RB, 128), jnp.bfloat16),
        in_specs=[pl.BlockSpec(memory_space=VMEM)] * 3,
        out_specs=pl.BlockSpec(memory_space=VMEM),
        compiler_params=pltpu.CompilerParams(vmem_limit_bytes=16 << 20),
        name="finish",
    )(total, row, col)


def local(amplitudes, integrals, amp_mask, int_mask, occ_row, occ_col, vir_energy):
    y, x, z, core = (lax.axis_index(name) for name in AXES)
    place = jnp.stack([y, x, z]).astype(jnp.int32)
    own, oth, near, up, down, over = prepare(place, amp_mask, int_mask, amplitudes, integrals)

    from_down = send(up, UP)
    from_up = send(down, DOWN)
    from_over = send(over, OVER)
    from_near = send(near, CROSS)
    p0 = send(own, PARTNER)
    x0 = send(follow(oth, p0), ACROSS)

    own_rest, oth_rest, b_here = gather(near, from_near, from_down, from_up, from_over, p0, x0)
    b_down = send(b_here, UP)
    b_up = send(b_here, DOWN)
    p1 = send(own_rest, PARTNER)
    c1 = send(oth_rest, CROSS)
    x1 = send(oth_rest, ACROSS)
    b_far0 = send(b_down[:128], UP)
    b_far1 = send(b_up[128:], DOWN)
    slabs = join(place, b_here, b_down, b_up, b_far0, b_far1)

    amps = (own, from_down, from_up, from_over, p0, p1, from_near, c1, x0, x1)
    keep_half = jnp.bitwise_xor(x // 2, core).astype(jnp.int32)
    give = arrange(place, (1 - keep_half)[None], amps)
    given = jnp.dot(slabs, give, preferred_element_type=jnp.float32)
    taken = send(given, SWAP)
    keep = arrange(place, keep_half[None], amps)

    def partial(spot):
        rows = slice(spot * 128, spot * 128 + 128)
        return jnp.dot(slabs[rows], keep, preferred_element_type=jnp.float32) + taken[rows]

    farthest = partial(0)
    ahead, behind = farthest[:64], farthest[64:]
    for step in range(3):
        ahead, behind = send(ahead, AHEAD), send(behind, BEHIND)
        if step == 0:
            ahead = jnp.pad(ahead, ((0, 64), (0, 0)))
            behind = jnp.pad(behind, ((64, 0), (0, 0)))
        ahead = partial(1 + 2 * step) + ahead
        behind = partial(2 + 2 * step) + behind
    cycle_sum = partial(7) + send(ahead, AHEAD) + send(behind, BEHIND)

    row_x = jnp.where(core == 0, x, 3 - x)
    row_occ = lax.dynamic_slice(occ_row, (4 * row_x,), (4,))
    row_vir = lax.dynamic_slice(vir_energy, (y, 0), (1, 128))
    row_energy = (row_vir - row_occ[:, None]).reshape(1, RB)
    col_y, col_x = slab_of(x, z)
    col_occ = lax.dynamic_slice(occ_col, (col_x,), (1,))
    col_energy = (lax.dynamic_slice(vir_energy, (col_y, 0), (1, 128)) - col_occ).reshape(128, 1)
    return send(finish(cycle_sum, row_energy, col_energy), HOME)


def solution(mesh):
    grid = Mesh(mesh.devices.reshape(NY, NX, NZ, NC), AXES)
    layout, rep = ("y", "x"), ("z", "core")
    placed = (P(rep, layout, None), P(rep, None, layout), P(), P(), P(), P(), P())
    return jax.shard_map(
        local, mesh=grid, in_specs=placed, out_specs=P(layout, rep), check_vma=False
    )
```

```python
import jax
import jax.numpy as jnp
from jax import lax
from jax.experimental import pallas as pl
from jax.experimental.pallas import tpu as pltpu
from jax.sharding import Mesh, PartitionSpec as P

AXES = ("y", "x", "z", "core")
NY, NX, NZ, NC = 4, 4, 8, 2
KD = 192
RB = 512
KT = 16 * KD
VMEM = pltpu.MemorySpace.VMEM


def pairs(to):
    out = []
    for y in range(NY):
        for x in range(NX):
            for z in range(NZ):
                for c in range(NC):
                    ty, tx, tz, tc = to(y, x, z, c)
                    src = ((y * NX + x) * NZ + z) * NC + c
                    dst = ((ty % NY * NX + tx % NX) * NZ + tz % NZ) * NC + tc % NC
                    out.append((src, dst))
    return out


UP = pairs(lambda y, x, z, c: (y + 1, x, z, c))
DOWN = pairs(lambda y, x, z, c: (y - 1, x, z, c))
OVER = pairs(lambda y, x, z, c: (y + 2, x, z, c))
PARTNER = pairs(lambda y, x, z, c: (y, 3 - x, z, c))
CROSS = pairs(lambda y, x, z, c: (y, x ^ 1, z, c))
ACROSS = pairs(lambda y, x, z, c: (y, x + 2, z, c))
AHEAD = pairs(lambda y, x, z, c: (y, x, z + 1, c))
BEHIND = pairs(lambda y, x, z, c: (y, x, z - 1, c))
SWAP = pairs(lambda y, x, z, c: (y, x, z, 1 - c))


def slab_of(x, z):
    return z // 2, 2 * (x // 2) + z % 2


def home(y, x, z, c):
    col_y, col_x = slab_of(x, z)
    return y, x if c == 0 else 3 - x, 2 * col_y + col_x // 2, col_x % 2


HOME = pairs(home)


def send(value, where):
    return lax.ppermute(value, AXES, where)


def prepare_kernel(
    place, amp_mask, int_mask, a_any, b_any, own, oth, near, up, down, over, a, b, scratch, sems
):
    y, x = place[0], place[1]
    block_q = 2 * y + x // 2
    low = jnp.minimum(x, 3 - x)
    turns = (y, lax.rem(y + 1, 4), lax.rem(y + 3, 4), lax.rem(y + 2, 4))
    moves = [pltpu.make_async_copy(b_any, b, sems.at[4])]
    for j, to_y in enumerate(turns):
        lanes = pl.ds(pl.multiple_of(to_y * 4 * RB, 4 * RB), 4 * RB)
        moves.append(pltpu.make_async_copy(a_any.at[:, :, lanes], a.at[j], sems.at[j]))
    for move in moves:
        move.start()
    moves[0].wait()
    for slab in range(16):
        keep = int_mask[y, slab // 2].astype(jnp.float32).astype(jnp.bfloat16)
        at = ((slab % 4) * 4 + slab // 4) * KD
        for k in range(3):
            scratch[pl.ds(at + k * 64, 64), :] = b[k, pl.ds(slab * 64, 64), :] * keep
    for j in range(KT // 128):
        near[pl.ds(0, 128), pl.ds(j * 128, 128)] = scratch[pl.ds(j * 128, 128), :].T
    for j, (first, second) in enumerate(
        ((own, oth), (up.at[0], up.at[1]), (down.at[0], down.at[1]), (over.at[0], over.at[1]))
    ):
        moves[1 + j].wait()
        keep = amp_mask[turns[j], block_q].astype(jnp.float32).astype(jnp.bfloat16)
        for dst, lo in ((first, low), (second, 1 - low)):
            for half in range(2):
                to_x = lo if half == 0 else 3 - lo
                start = pl.multiple_of(to_x * RB, RB)
                for k in range(3):
                    value = a[j, k, :, pl.ds(start, RB)] * keep
                    dst[pl.ds(k * 64, 64), pl.ds(half * RB, RB)] = value
                    if dst is oth:
                        near[pl.ds(128, 64), pl.ds((2 * k + half) * RB, RB)] = value


def prepare(place, amp_mask, int_mask, a, b):
    piece = jax.ShapeDtypeStruct((KD, 2 * RB), jnp.bfloat16)
    two = jax.ShapeDtypeStruct((2, KD, 2 * RB), jnp.bfloat16)
    near = jax.ShapeDtypeStruct((KD, KT), jnp.bfloat16)
    anywhere = pl.BlockSpec(memory_space=pl.ANY)
    vmem = pl.BlockSpec(memory_space=VMEM)
    return pl.pallas_call(
        prepare_kernel,
        out_shape=(piece, piece, near, two, two, two),
        grid_spec=pltpu.PrefetchScalarGridSpec(
            num_scalar_prefetch=3,
            grid=(1,),
            in_specs=[anywhere, anywhere],
            out_specs=(vmem,) * 6,
            scratch_shapes=[
                pltpu.VMEM((4, 3, 64, 4 * RB), jnp.bfloat16),
                pltpu.VMEM((3, 1024, 128), jnp.bfloat16),
                pltpu.VMEM((KT, 128), jnp.bfloat16),
                pltpu.SemaphoreType.DMA((5,)),
            ],
        ),
        compiler_params=pltpu.CompilerParams(vmem_limit_bytes=55 << 20),
        cost_estimate=pl.CostEstimate(flops=0, bytes_accessed=8 << 20, transcendentals=0),
        name="prepare",
    )(place, amp_mask, int_mask.T, a, b)


def follow_kernel(value, after, out):
    del after
    out[...] = value[...]


def follow(value, after):
    vmem = pl.BlockSpec(memory_space=VMEM)
    return pl.pallas_call(
        follow_kernel,
        out_shape=jax.ShapeDtypeStruct(value.shape, value.dtype),
        in_specs=[vmem, pl.BlockSpec(memory_space=pl.ANY)],
        out_specs=vmem,
        compiler_params=pltpu.CompilerParams(vmem_limit_bytes=4 << 20),
        cost_estimate=pl.CostEstimate(flops=0, bytes_accessed=1 << 20, transcendentals=0),
        name="follow",
    )(value, after)


def gather_kernel(
    near, from_near, down, up, over, own, p0, x0, own_rest, oth_rest, b_here, early
):
    for j, ref in enumerate((down, up, over)):
        own_rest[j] = ref[0]
        oth_rest[j] = ref[1]
    b_here[pl.ds(0, 128), :] = near[...]
    b_here[pl.ds(128, 128), :] = from_near[pl.ds(0, 128), :]
    for j, ref in ((0, own), (1, p0), (3, x0)):
        early[j] = ref[...]
    for k in range(3):
        early[2, pl.ds(k * 64, 64), :] = from_near[pl.ds(128, 64), pl.ds(k * 2 * RB, 2 * RB)]


def gather(*parts):
    def stack(n):
        return jax.ShapeDtypeStruct((n, KD, 2 * RB), jnp.bfloat16)

    vmem = pl.BlockSpec(memory_space=VMEM)
    return pl.pallas_call(
        gather_kernel,
        out_shape=(stack(3), stack(3), jax.ShapeDtypeStruct((256, KT), jnp.bfloat16), stack(4)),
        grid=(1,),
        in_specs=[pl.BlockSpec((128, KT), lambda i: (0, 0))] + [vmem] * 7,
        out_specs=(vmem,) * 4,
        compiler_params=pltpu.CompilerParams(vmem_limit_bytes=20 << 20),
        cost_estimate=pl.CostEstimate(flops=0, bytes_accessed=10 << 20, transcendentals=0),
        name="gather",
    )(*parts)


def run(moves, sems):
    copies = [pltpu.make_async_copy(src, dst, sems.at[i]) for i, (src, dst) in enumerate(moves)]
    for copy in copies:
        copy.start()
    for copy in copies:
        copy.wait()


def join_kernel(place, here, down, up, far0, far1, out, sems):
    y, odd, z = place[0], lax.rem(place[1], 2), place[2]
    moves = []
    for turn, first, second in ((0, here, here), (3, down, down), (1, up, up), (2, far0, far1)):
        at = lax.rem(y + turn, 4) * 2
        skip = 0 if first is far0 else 128
        for bit, src in ((odd, first.at[pl.ds(0, 128), :]), (1 - odd, second.at[pl.ds(skip, 128), :])):
            ahead = lax.rem(at + bit - z + 8, 8)
            spot = jnp.where(ahead == 0, 7, jnp.where(ahead < 5, 7 - 2 * ahead, 2 * ahead - 8))
            spot = jnp.maximum(spot, 0)
            moves.append((src, out.at[pl.ds(pl.multiple_of(spot * 128, 128), 128), :]))
    run(moves, sems)


def join(place, *parts):
    return pl.pallas_call(
        join_kernel,
        out_shape=jax.ShapeDtypeStruct((1024, KT), jnp.bfloat16),
        grid_spec=pltpu.PrefetchScalarGridSpec(
            num_scalar_prefetch=1,
            grid=(1,),
            in_specs=[pl.BlockSpec(memory_space=pl.ANY)] * 5,
            out_specs=pl.BlockSpec(memory_space=VMEM),
            scratch_shapes=[pltpu.SemaphoreType.DMA((8,))],
        ),
        compiler_params=pltpu.CompilerParams(vmem_limit_bytes=16 << 20),
        cost_estimate=pl.CostEstimate(flops=0, bytes_accessed=6 << 20, transcendentals=0),
        name="join",
    )(place, *parts)


def arrange_kernel(place, half, early, own_rest, p1, c1, x1, out, sems):
    y, x = place[0], place[1]
    lanes = pl.ds(pl.multiple_of(half[0] * RB, RB), RB)
    around = (lax.rem(y + 3, 4), lax.rem(y + 1, 4), lax.rem(y + 2, 4))
    sources = (x, 3 - x, x + 1 - 2 * lax.rem(x, 2), lax.rem(x + 2, 4))
    moves = []
    for j, (rest, from_x) in enumerate(zip((own_rest, p1, c1, x1), sources)):
        for ref, from_y in ((early.at[j], y), *((rest.at[i], at) for i, at in enumerate(around))):
            at = pl.multiple_of((from_x * 4 + from_y) * KD, KD)
            moves.append((ref.at[:, lanes], out.at[pl.ds(at, KD), :]))
    run(moves, sems)


def arrange(place, half, amps):
    return pl.pallas_call(
        arrange_kernel,
        out_shape=jax.ShapeDtypeStruct((KT, RB), jnp.bfloat16),
        grid_spec=pltpu.PrefetchScalarGridSpec(
            num_scalar_prefetch=2,
            grid=(1,),
            in_specs=[pl.BlockSpec(memory_space=pl.ANY)] * 5,
            out_specs=pl.BlockSpec(memory_space=VMEM),
            scratch_shapes=[pltpu.SemaphoreType.DMA((16,))],
        ),
        compiler_params=pltpu.CompilerParams(vmem_limit_bytes=16 << 20),
        cost_estimate=pl.CostEstimate(flops=0, bytes_accessed=6 << 20, transcendentals=0),
        name="arrange",
    )(place, half, *amps)


def finish_kernel(total, row, col, out):
    out[...] = (total[...] / -(row[...] + col[...])).T.astype(jnp.bfloat16)


def finish(total, row, col):
    return pl.pallas_call(
        finish_kernel,
        out_shape=jax.ShapeDtypeStruct((RB, 128), jnp.bfloat16),
        in_specs=[pl.BlockSpec(memory_space=VMEM)] * 3,
        out_specs=pl.BlockSpec(memory_space=VMEM),
        compiler_params=pltpu.CompilerParams(vmem_limit_bytes=16 << 20),
        name="finish",
    )(total, row, col)


def local(amplitudes, integrals, amp_mask, int_mask, occ_row, occ_col, vir_energy):
    y, x, z, core = (lax.axis_index(name) for name in AXES)
    place = jnp.stack([y, x, z]).astype(jnp.int32)
    own, oth, near, up, down, over = prepare(place, amp_mask, int_mask, amplitudes, integrals)

    from_down = send(up, UP)
    from_up = send(down, DOWN)
    from_over = send(over, OVER)
    from_near = send(near, CROSS)
    p0 = send(own, PARTNER)
    x0 = send(follow(oth, p0), ACROSS)

    own_rest, oth_rest, b_here, early = gather(
        near, from_near, from_down, from_up, from_over, own, p0, x0
    )
    b_down = send(b_here, UP)
    b_up = send(b_here, DOWN)
    p1 = send(own_rest, PARTNER)
    c1 = send(oth_rest, CROSS)
    x1 = send(oth_rest, ACROSS)
    b_far0 = send(b_down[:128], UP)
    b_far1 = send(b_up[128:], DOWN)
    slabs = join(place, b_here, b_down, b_up, b_far0, b_far1)

    amps = (early, own_rest, p1, c1, x1)
    keep_half = jnp.bitwise_xor(x // 2, core).astype(jnp.int32)
    give = arrange(place, (1 - keep_half)[None], amps)
    given = jnp.dot(slabs, give, preferred_element_type=jnp.float32)
    taken = send(given, SWAP)
    keep = arrange(place, keep_half[None], amps)

    def partial(spot):
        rows = slice(spot * 128, spot * 128 + 128)
        return jnp.dot(slabs[rows], keep, preferred_element_type=jnp.float32) + taken[rows]

    farthest = partial(0)
    ahead, behind = farthest[:64], farthest[64:]
    for step in range(3):
        ahead, behind = send(ahead, AHEAD), send(behind, BEHIND)
        if step == 0:
            ahead = jnp.pad(ahead, ((0, 64), (0, 0)))
            behind = jnp.pad(behind, ((64, 0), (0, 0)))
        ahead = partial(1 + 2 * step) + ahead
        behind = partial(2 + 2 * step) + behind
    cycle_sum = partial(7) + send(ahead, AHEAD) + send(behind, BEHIND)

    row_x = jnp.where(core == 0, x, 3 - x)
    row_occ = lax.dynamic_slice(occ_row, (4 * row_x,), (4,))
    row_vir = lax.dynamic_slice(vir_energy, (y, 0), (1, 128))
    row_energy = (row_vir - row_occ[:, None]).reshape(1, RB)
    col_y, col_x = slab_of(x, z)
    col_occ = lax.dynamic_slice(occ_col, (col_x,), (1,))
    col_energy = (lax.dynamic_slice(vir_energy, (col_y, 0), (1, 128)) - col_occ).reshape(128, 1)
    return send(finish(cycle_sum, row_energy, col_energy), HOME)


def solution(mesh):
    grid = Mesh(mesh.devices.reshape(NY, NX, NZ, NC), AXES)
    layout, rep = ("y", "x"), ("z", "core")
    placed = (P(rep, layout, None), P(rep, None, layout), P(), P(), P(), P(), P())
    return jax.shard_map(
        local, mesh=grid, in_specs=placed, out_specs=P(layout, rep), check_vma=False
    )
```

```python
import functools

import jax
import jax.numpy as jnp
from jax import lax
from jax.experimental import pallas as pl
from jax.experimental.pallas import tpu as pltpu
from jax.sharding import Mesh, PartitionSpec as P

AXES = ("y", "x", "z", "core")
NY, NX, NZ, NC = 4, 4, 8, 2
KD = 192
RB = 512
KT = 16 * KD
VMEM = pltpu.MemorySpace.VMEM


def pairs(to):
    out = []
    for y in range(NY):
        for x in range(NX):
            for z in range(NZ):
                for c in range(NC):
                    ty, tx, tz, tc = to(y, x, z, c)
                    src = ((y * NX + x) * NZ + z) * NC + c
                    dst = ((ty % NY * NX + tx % NX) * NZ + tz % NZ) * NC + tc % NC
                    out.append((src, dst))
    return out


UP = pairs(lambda y, x, z, c: (y + 1, x, z, c))
DOWN = pairs(lambda y, x, z, c: (y - 1, x, z, c))
OVER = pairs(lambda y, x, z, c: (y + 2, x, z, c))
PARTNER = pairs(lambda y, x, z, c: (y, 3 - x, z, c))
CROSS = pairs(lambda y, x, z, c: (y, x ^ 1, z, c))
ACROSS = pairs(lambda y, x, z, c: (y, x + 2, z, c))
AHEAD = pairs(lambda y, x, z, c: (y, x, z + 1, c))
BEHIND = pairs(lambda y, x, z, c: (y, x, z - 1, c))
SWAP = pairs(lambda y, x, z, c: (y, x, z, 1 - c))


def slab_of(x, z):
    return z // 2, 2 * (x // 2) + z % 2


def home(y, x, z, c):
    col_y, col_x = slab_of(x, z)
    return y, x if c == 0 else 3 - x, 2 * col_y + col_x // 2, col_x % 2


HOME = pairs(home)


def send(value, where):
    return lax.ppermute(value, AXES, where)


def prepare_kernel(
    place, amp_mask, int_mask, a_any, b_any, own, oth, near, up, down, over, a, b, scratch, sems
):
    y, x = place[0], place[1]
    block_q = 2 * y + x // 2
    low = jnp.minimum(x, 3 - x)
    turns = (y, lax.rem(y + 1, 4), lax.rem(y + 3, 4), lax.rem(y + 2, 4))
    moves = [pltpu.make_async_copy(b_any, b, sems.at[4])]
    for j, to_y in enumerate(turns):
        lanes = pl.ds(pl.multiple_of(to_y * 4 * RB, 4 * RB), 4 * RB)
        moves.append(pltpu.make_async_copy(a_any.at[:, :, lanes], a.at[j], sems.at[j]))
    for move in moves:
        move.start()
    moves[0].wait()
    for slab in range(16):
        keep = int_mask[y, slab // 2].astype(jnp.float32).astype(jnp.bfloat16)
        at = ((slab % 4) * 4 + slab // 4) * KD
        for k in range(3):
            scratch[pl.ds(at + k * 64, 64), :] = b[k, pl.ds(slab * 64, 64), :] * keep
    for j in range(KT // 128):
        near[pl.ds(0, 128), pl.ds(j * 128, 128)] = scratch[pl.ds(j * 128, 128), :].T
    for j, (first, second) in enumerate(
        ((own, oth), (up.at[0], up.at[1]), (down.at[0], down.at[1]), (over.at[0], over.at[1]))
    ):
        moves[1 + j].wait()
        keep = amp_mask[turns[j], block_q].astype(jnp.float32).astype(jnp.bfloat16)
        for dst, lo in ((first, low), (second, 1 - low)):
            for half in range(2):
                to_x = lo if half == 0 else 3 - lo
                start = pl.multiple_of(to_x * RB, RB)
                for k in range(3):
                    value = a[j, k, :, pl.ds(start, RB)] * keep
                    dst[pl.ds(k * 64, 64), pl.ds(half * RB, RB)] = value
                    if dst is oth:
                        near[pl.ds(128, 64), pl.ds((2 * k + half) * RB, RB)] = value


def prepare(place, amp_mask, int_mask, a, b):
    piece = jax.ShapeDtypeStruct((KD, 2 * RB), jnp.bfloat16)
    two = jax.ShapeDtypeStruct((2, KD, 2 * RB), jnp.bfloat16)
    near = jax.ShapeDtypeStruct((KD, KT), jnp.bfloat16)
    anywhere = pl.BlockSpec(memory_space=pl.ANY)
    vmem = pl.BlockSpec(memory_space=VMEM)
    return pl.pallas_call(
        prepare_kernel,
        out_shape=(piece, piece, near, two, two, two),
        grid_spec=pltpu.PrefetchScalarGridSpec(
            num_scalar_prefetch=3,
            grid=(1,),
            in_specs=[anywhere, anywhere],
            out_specs=(vmem,) * 6,
            scratch_shapes=[
                pltpu.VMEM((4, 3, 64, 4 * RB), jnp.bfloat16),
                pltpu.VMEM((3, 1024, 128), jnp.bfloat16),
                pltpu.VMEM((KT, 128), jnp.bfloat16),
                pltpu.SemaphoreType.DMA((5,)),
            ],
        ),
        compiler_params=pltpu.CompilerParams(vmem_limit_bytes=55 << 20),
        cost_estimate=pl.CostEstimate(flops=0, bytes_accessed=8 << 20, transcendentals=0),
        name="prepare",
    )(place, amp_mask, int_mask.T, a, b)


def follow_kernel(value, after, out):
    del after
    out[...] = value[...]


def follow(value, after):
    vmem = pl.BlockSpec(memory_space=VMEM)
    return pl.pallas_call(
        follow_kernel,
        out_shape=jax.ShapeDtypeStruct(value.shape, value.dtype),
        in_specs=[vmem, pl.BlockSpec(memory_space=pl.ANY)],
        out_specs=vmem,
        compiler_params=pltpu.CompilerParams(vmem_limit_bytes=4 << 20),
        cost_estimate=pl.CostEstimate(flops=0, bytes_accessed=1 << 20, transcendentals=0),
        name="follow",
    )(value, after)


def gather_kernel(
    near, from_near, down, up, over, own, p0, x0, own_rest, oth_rest, b_here, early
):
    for j, ref in enumerate((down, up, over)):
        own_rest[j] = ref[0]
        oth_rest[j] = ref[1]
    b_here[pl.ds(0, 128), :] = near[...]
    b_here[pl.ds(128, 128), :] = from_near[pl.ds(0, 128), :]
    for j, ref in ((0, own), (1, p0), (3, x0)):
        early[j] = ref[...]
    for k in range(3):
        early[2, pl.ds(k * 64, 64), :] = from_near[pl.ds(128, 64), pl.ds(k * 2 * RB, 2 * RB)]


def gather(*parts):
    def stack(n):
        return jax.ShapeDtypeStruct((n, KD, 2 * RB), jnp.bfloat16)

    vmem = pl.BlockSpec(memory_space=VMEM)
    return pl.pallas_call(
        gather_kernel,
        out_shape=(stack(3), stack(3), jax.ShapeDtypeStruct((256, KT), jnp.bfloat16), stack(4)),
        grid=(1,),
        in_specs=[pl.BlockSpec((128, KT), lambda i: (0, 0))] + [vmem] * 7,
        out_specs=(vmem,) * 4,
        compiler_params=pltpu.CompilerParams(vmem_limit_bytes=20 << 20),
        cost_estimate=pl.CostEstimate(flops=0, bytes_accessed=10 << 20, transcendentals=0),
        name="gather",
    )(*parts)


def run(moves, sems):
    copies = [pltpu.make_async_copy(src, dst, sems.at[i]) for i, (src, dst) in enumerate(moves)]
    for copy in copies:
        copy.start()
    for copy in copies:
        copy.wait()


def join_kernel(place, here, down, up, far0, far1, out, sems):
    y, odd, z = place[0], lax.rem(place[1], 2), place[2]
    moves = []
    for turn, first, second in ((0, here, here), (3, down, down), (1, up, up), (2, far0, far1)):
        at = lax.rem(y + turn, 4) * 2
        skip = 0 if first is far0 else 128
        for bit, src in ((odd, first.at[pl.ds(0, 128), :]), (1 - odd, second.at[pl.ds(skip, 128), :])):
            ahead = lax.rem(at + bit - z + 8, 8)
            spot = jnp.where(ahead == 0, 7, jnp.where(ahead < 5, 7 - 2 * ahead, 2 * ahead - 8))
            spot = jnp.maximum(spot, 0)
            moves.append((src, out.at[pl.ds(pl.multiple_of(spot * 128, 128), 128), :]))
    run(moves, sems)


def join(place, *parts):
    return pl.pallas_call(
        join_kernel,
        out_shape=jax.ShapeDtypeStruct((1024, KT), jnp.bfloat16),
        grid_spec=pltpu.PrefetchScalarGridSpec(
            num_scalar_prefetch=1,
            grid=(1,),
            in_specs=[pl.BlockSpec(memory_space=pl.ANY)] * 5,
            out_specs=pl.BlockSpec(memory_space=VMEM),
            scratch_shapes=[pltpu.SemaphoreType.DMA((8,))],
        ),
        compiler_params=pltpu.CompilerParams(vmem_limit_bytes=16 << 20),
        cost_estimate=pl.CostEstimate(flops=0, bytes_accessed=6 << 20, transcendentals=0),
        name="join",
    )(place, *parts)


def arrange_kernel(place, half, early, own_rest, p1, c1, x1, out, sems):
    y, x = place[0], place[1]
    lanes = pl.ds(pl.multiple_of(half[0] * RB, RB), RB)
    around = (lax.rem(y + 3, 4), lax.rem(y + 1, 4), lax.rem(y + 2, 4))
    sources = (x, 3 - x, x + 1 - 2 * lax.rem(x, 2), lax.rem(x + 2, 4))
    moves = []
    for j, (rest, from_x) in enumerate(zip((own_rest, p1, c1, x1), sources)):
        for ref, from_y in ((early.at[j], y), *((rest.at[i], at) for i, at in enumerate(around))):
            at = pl.multiple_of((from_x * 4 + from_y) * KD, KD)
            moves.append((ref.at[:, lanes], out.at[pl.ds(at, KD), :]))
    run(moves, sems)


def arrange(place, half, amps):
    return pl.pallas_call(
        arrange_kernel,
        out_shape=jax.ShapeDtypeStruct((KT, RB), jnp.bfloat16),
        grid_spec=pltpu.PrefetchScalarGridSpec(
            num_scalar_prefetch=2,
            grid=(1,),
            in_specs=[pl.BlockSpec(memory_space=pl.ANY)] * 5,
            out_specs=pl.BlockSpec(memory_space=VMEM),
            scratch_shapes=[pltpu.SemaphoreType.DMA((16,))],
        ),
        compiler_params=pltpu.CompilerParams(vmem_limit_bytes=16 << 20),
        cost_estimate=pl.CostEstimate(flops=0, bytes_accessed=6 << 20, transcendentals=0),
        name="arrange",
    )(place, half, *amps)


def merge_kernel(mine, got, out, *, first):
    if got.shape[0] == mine.shape[0]:
        out[...] = mine[...] + got[...]
    else:
        rest = 64 - first
        out[pl.ds(first, 64), :] = mine[pl.ds(first, 64), :] + got[...]
        out[pl.ds(rest, 64), :] = mine[pl.ds(rest, 64), :]


def merge(others, spot, got, first):
    vmem = pl.BlockSpec(memory_space=VMEM)
    return pl.pallas_call(
        functools.partial(merge_kernel, first=first),
        out_shape=jax.ShapeDtypeStruct((128, RB), jnp.float32),
        grid=(1,),
        in_specs=[pl.BlockSpec((128, RB), lambda i: (spot, 0)), vmem],
        out_specs=vmem,
        compiler_params=pltpu.CompilerParams(vmem_limit_bytes=4 << 20),
        cost_estimate=pl.CostEstimate(flops=0, bytes_accessed=1 << 20, transcendentals=0),
        name="merge",
    )(others, got)


def finish_kernel(mine, ahead, behind, row, col, out):
    total = mine[...] + ahead[...] + behind[...]
    out[...] = (total / -(row[...] + col[...])).T.astype(jnp.bfloat16)


def finish(*parts):
    vmem = pl.BlockSpec(memory_space=VMEM)
    return pl.pallas_call(
        finish_kernel,
        out_shape=jax.ShapeDtypeStruct((RB, 128), jnp.bfloat16),
        grid=(1,),
        in_specs=[pl.BlockSpec((128, RB), lambda i: (6, 0))] + [vmem] * 4,
        out_specs=vmem,
        compiler_params=pltpu.CompilerParams(vmem_limit_bytes=8 << 20),
        name="finish",
    )(*parts)


def local(amplitudes, integrals, amp_mask, int_mask, occ_row, occ_col, vir_energy):
    y, x, z, core = (lax.axis_index(name) for name in AXES)
    place = jnp.stack([y, x, z]).astype(jnp.int32)
    own, oth, near, up, down, over = prepare(place, amp_mask, int_mask, amplitudes, integrals)

    from_down = send(up, UP)
    from_up = send(down, DOWN)
    from_over = send(over, OVER)
    from_near = send(near, CROSS)
    p0 = send(own, PARTNER)
    x0 = send(follow(oth, p0), ACROSS)

    own_rest, oth_rest, b_here, early = gather(
        near, from_near, from_down, from_up, from_over, own, p0, x0
    )
    b_down = send(b_here, UP)
    b_up = send(b_here, DOWN)
    p1 = send(own_rest, PARTNER)
    c1 = send(oth_rest, CROSS)
    x1 = send(oth_rest, ACROSS)
    b_far0 = send(b_down[:128], UP)
    b_far1 = send(b_up[128:], DOWN)
    slabs = join(place, b_here, b_down, b_up, b_far0, b_far1)

    amps = (early, own_rest, p1, c1, x1)
    keep_half = jnp.bitwise_xor(x // 2, core).astype(jnp.int32)
    give = arrange(place, (1 - keep_half)[None], amps)
    given = jnp.dot(slabs, give, preferred_element_type=jnp.float32)
    taken = send(given, SWAP)
    keep = arrange(place, keep_half[None], amps)

    farthest = jnp.dot(slabs[:128], keep, preferred_element_type=jnp.float32) + taken[:128]
    others = jnp.dot(slabs[128:], keep, preferred_element_type=jnp.float32) + taken[128:]
    ahead, behind = farthest[:64], farthest[64:]
    for step in range(3):
        ahead, behind = send(ahead, AHEAD), send(behind, BEHIND)
        ahead = merge(others, 2 * step, ahead, 0)
        behind = merge(others, 1 + 2 * step, behind, 64)
    ahead, behind = send(ahead, AHEAD), send(behind, BEHIND)

    row_x = jnp.where(core == 0, x, 3 - x)
    row_occ = lax.dynamic_slice(occ_row, (4 * row_x,), (4,))
    row_vir = lax.dynamic_slice(vir_energy, (y, 0), (1, 128))
    row_energy = (row_vir - row_occ[:, None]).reshape(1, RB)
    col_y, col_x = slab_of(x, z)
    col_occ = lax.dynamic_slice(occ_col, (col_x,), (1,))
    col_energy = (lax.dynamic_slice(vir_energy, (col_y, 0), (1, 128)) - col_occ).reshape(128, 1)
    return send(finish(others, ahead, behind, row_energy, col_energy), HOME)


def solution(mesh):
    grid = Mesh(mesh.devices.reshape(NY, NX, NZ, NC), AXES)
    layout, rep = ("y", "x"), ("z", "core")
    placed = (P(rep, layout, None), P(rep, None, layout), P(), P(), P(), P(), P())
    return jax.shard_map(
        local, mesh=grid, in_specs=placed, out_specs=P(layout, rep), check_vma=False
    )
```

```python
import functools

import jax
import jax.numpy as jnp
from jax import lax
from jax.experimental import pallas as pl
from jax.experimental.pallas import tpu as pltpu
from jax.sharding import Mesh, PartitionSpec as P

AXES = ("y", "x", "z", "core")
NY, NX, NZ, NC = 4, 4, 8, 2
KD = 192
RB = 512
KT = 16 * KD
VMEM = pltpu.MemorySpace.VMEM


def pairs(to):
    out = []
    for y in range(NY):
        for x in range(NX):
            for z in range(NZ):
                for c in range(NC):
                    ty, tx, tz, tc = to(y, x, z, c)
                    src = ((y * NX + x) * NZ + z) * NC + c
                    dst = ((ty % NY * NX + tx % NX) * NZ + tz % NZ) * NC + tc % NC
                    out.append((src, dst))
    return out


UP = pairs(lambda y, x, z, c: (y + 1, x, z, c))
DOWN = pairs(lambda y, x, z, c: (y - 1, x, z, c))
OVER = pairs(lambda y, x, z, c: (y + 2, x, z, c))
PARTNER = pairs(lambda y, x, z, c: (y, 3 - x, z, c))
CROSS = pairs(lambda y, x, z, c: (y, x ^ 1, z, c))
ACROSS = pairs(lambda y, x, z, c: (y, x + 2, z, c))
AHEAD = pairs(lambda y, x, z, c: (y, x, z + 1, c))
BEHIND = pairs(lambda y, x, z, c: (y, x, z - 1, c))
SWAP = pairs(lambda y, x, z, c: (y, x, z, 1 - c))


def slab_of(x, z):
    return z // 2, 2 * (x // 2) + z % 2


def home(y, x, z, c):
    col_y, col_x = slab_of(x, z)
    return y, x if c == 0 else 3 - x, 2 * col_y + col_x // 2, col_x % 2


HOME = pairs(home)


def send(value, where):
    return lax.ppermute(value, AXES, where)


def prepare_kernel(
    amp_mask, int_mask, a_any, b_any, own, oth, near, up, down, over, a, b, scratch, sems
):
    y, x = lax.axis_index("y"), lax.axis_index("x")
    block_q = 2 * y + x // 2
    low = jnp.minimum(x, 3 - x)
    turns = (y, lax.rem(y + 1, 4), lax.rem(y + 3, 4), lax.rem(y + 2, 4))
    moves = [pltpu.make_async_copy(b_any, b, sems.at[4])]
    for j, to_y in enumerate(turns):
        lanes = pl.ds(pl.multiple_of(to_y * 4 * RB, 4 * RB), 4 * RB)
        moves.append(pltpu.make_async_copy(a_any.at[:, :, lanes], a.at[j], sems.at[j]))
    for move in moves:
        move.start()
    moves[0].wait()
    for slab in range(16):
        keep = int_mask[y, slab // 2].astype(jnp.float32).astype(jnp.bfloat16)
        at = ((slab % 4) * 4 + slab // 4) * KD
        for k in range(3):
            scratch[pl.ds(at + k * 64, 64), :] = b[k, pl.ds(slab * 64, 64), :] * keep
    for j in range(KT // 128):
        near[pl.ds(0, 128), pl.ds(j * 128, 128)] = scratch[pl.ds(j * 128, 128), :].T
    for j, (first, second) in enumerate(
        ((own, oth), (up.at[0], up.at[1]), (down.at[0], down.at[1]), (over.at[0], over.at[1]))
    ):
        moves[1 + j].wait()
        keep = amp_mask[turns[j], block_q].astype(jnp.float32).astype(jnp.bfloat16)
        for dst, lo in ((first, low), (second, 1 - low)):
            for half in range(2):
                to_x = lo if half == 0 else 3 - lo
                start = pl.multiple_of(to_x * RB, RB)
                for k in range(3):
                    value = a[j, k, :, pl.ds(start, RB)] * keep
                    dst[pl.ds(k * 64, 64), pl.ds(half * RB, RB)] = value
                    if dst is oth:
                        near[pl.ds(128, 64), pl.ds((2 * k + half) * RB, RB)] = value


def prepare(amp_mask, int_mask, a, b):
    piece = jax.ShapeDtypeStruct((KD, 2 * RB), jnp.bfloat16)
    two = jax.ShapeDtypeStruct((2, KD, 2 * RB), jnp.bfloat16)
    near = jax.ShapeDtypeStruct((KD, KT), jnp.bfloat16)
    anywhere = pl.BlockSpec(memory_space=pl.ANY)
    vmem = pl.BlockSpec(memory_space=VMEM)
    return pl.pallas_call(
        prepare_kernel,
        out_shape=(piece, piece, near, two, two, two),
        grid_spec=pltpu.PrefetchScalarGridSpec(
            num_scalar_prefetch=2,
            grid=(1,),
            in_specs=[anywhere, anywhere],
            out_specs=(vmem,) * 6,
            scratch_shapes=[
                pltpu.VMEM((4, 3, 64, 4 * RB), jnp.bfloat16),
                pltpu.VMEM((3, 1024, 128), jnp.bfloat16),
                pltpu.VMEM((KT, 128), jnp.bfloat16),
                pltpu.SemaphoreType.DMA((5,)),
            ],
        ),
        compiler_params=pltpu.CompilerParams(vmem_limit_bytes=55 << 20),
        cost_estimate=pl.CostEstimate(flops=0, bytes_accessed=8 << 20, transcendentals=0),
        name="prepare",
    )(amp_mask, int_mask.T, a, b)


def follow_kernel(value, after, out):
    del after
    out[...] = value[...]


def follow(value, after):
    vmem = pl.BlockSpec(memory_space=VMEM)
    return pl.pallas_call(
        follow_kernel,
        out_shape=jax.ShapeDtypeStruct(value.shape, value.dtype),
        in_specs=[vmem, pl.BlockSpec(memory_space=pl.ANY)],
        out_specs=vmem,
        compiler_params=pltpu.CompilerParams(vmem_limit_bytes=4 << 20),
        cost_estimate=pl.CostEstimate(flops=0, bytes_accessed=1 << 20, transcendentals=0),
        name="follow",
    )(value, after)


def gather_kernel(
    near, from_near, down, up, over, own, p0, x0, own_rest, oth_rest, b_here, early
):
    for j, ref in enumerate((down, up, over)):
        own_rest[j] = ref[0]
        oth_rest[j] = ref[1]
    b_here[pl.ds(0, 128), :] = near[...]
    b_here[pl.ds(128, 128), :] = from_near[pl.ds(0, 128), :]
    for j, ref in ((0, own), (1, p0), (3, x0)):
        early[j] = ref[...]
    for k in range(3):
        early[2, pl.ds(k * 64, 64), :] = from_near[pl.ds(128, 64), pl.ds(k * 2 * RB, 2 * RB)]


def gather(*parts):
    def stack(n):
        return jax.ShapeDtypeStruct((n, KD, 2 * RB), jnp.bfloat16)

    vmem = pl.BlockSpec(memory_space=VMEM)
    return pl.pallas_call(
        gather_kernel,
        out_shape=(stack(3), stack(3), jax.ShapeDtypeStruct((256, KT), jnp.bfloat16), stack(4)),
        grid=(1,),
        in_specs=[pl.BlockSpec((128, KT), lambda i: (0, 0))] + [vmem] * 7,
        out_specs=(vmem,) * 4,
        compiler_params=pltpu.CompilerParams(vmem_limit_bytes=20 << 20),
        cost_estimate=pl.CostEstimate(flops=0, bytes_accessed=10 << 20, transcendentals=0),
        name="gather",
    )(*parts)


def run(moves, sems):
    copies = [pltpu.make_async_copy(src, dst, sems.at[i]) for i, (src, dst) in enumerate(moves)]
    for copy in copies:
        copy.start()
    for copy in copies:
        copy.wait()


def join_kernel(place, here, down, up, far0, far1, out, sems):
    y, odd, z = place[0], lax.rem(place[1], 2), place[2]
    moves = []
    for turn, first, second in ((0, here, here), (3, down, down), (1, up, up), (2, far0, far1)):
        at = lax.rem(y + turn, 4) * 2
        skip = 0 if first is far0 else 128
        for bit, src in ((odd, first.at[pl.ds(0, 128), :]), (1 - odd, second.at[pl.ds(skip, 128), :])):
            ahead = lax.rem(at + bit - z + 8, 8)
            spot = jnp.where(ahead == 0, 7, jnp.where(ahead < 5, 7 - 2 * ahead, 2 * ahead - 8))
            spot = jnp.maximum(spot, 0)
            moves.append((src, out.at[pl.ds(pl.multiple_of(spot * 128, 128), 128), :]))
    run(moves, sems)


def join(place, *parts):
    return pl.pallas_call(
        join_kernel,
        out_shape=jax.ShapeDtypeStruct((1024, KT), jnp.bfloat16),
        grid_spec=pltpu.PrefetchScalarGridSpec(
            num_scalar_prefetch=1,
            grid=(1,),
            in_specs=[pl.BlockSpec(memory_space=pl.ANY)] * 5,
            out_specs=pl.BlockSpec(memory_space=VMEM),
            scratch_shapes=[pltpu.SemaphoreType.DMA((8,))],
        ),
        compiler_params=pltpu.CompilerParams(vmem_limit_bytes=16 << 20),
        cost_estimate=pl.CostEstimate(flops=0, bytes_accessed=6 << 20, transcendentals=0),
        name="join",
    )(place, *parts)


def arrange_kernel(place, half, early, own_rest, p1, c1, x1, out, sems):
    y, x = place[0], place[1]
    lanes = pl.ds(pl.multiple_of(half[0] * RB, RB), RB)
    around = (lax.rem(y + 3, 4), lax.rem(y + 1, 4), lax.rem(y + 2, 4))
    sources = (x, 3 - x, x + 1 - 2 * lax.rem(x, 2), lax.rem(x + 2, 4))
    moves = []
    for j, (rest, from_x) in enumerate(zip((own_rest, p1, c1, x1), sources)):
        for ref, from_y in ((early.at[j], y), *((rest.at[i], at) for i, at in enumerate(around))):
            at = pl.multiple_of((from_x * 4 + from_y) * KD, KD)
            moves.append((ref.at[:, lanes], out.at[pl.ds(at, KD), :]))
    run(moves, sems)


def arrange(place, half, amps):
    return pl.pallas_call(
        arrange_kernel,
        out_shape=jax.ShapeDtypeStruct((KT, RB), jnp.bfloat16),
        grid_spec=pltpu.PrefetchScalarGridSpec(
            num_scalar_prefetch=2,
            grid=(1,),
            in_specs=[pl.BlockSpec(memory_space=pl.ANY)] * 5,
            out_specs=pl.BlockSpec(memory_space=VMEM),
            scratch_shapes=[pltpu.SemaphoreType.DMA((16,))],
        ),
        compiler_params=pltpu.CompilerParams(vmem_limit_bytes=16 << 20),
        cost_estimate=pl.CostEstimate(flops=0, bytes_accessed=6 << 20, transcendentals=0),
        name="arrange",
    )(place, half, *amps)


def merge_kernel(mine, got, out, *, first):
    if got.shape[0] == mine.shape[0]:
        out[...] = mine[...] + got[...]
    else:
        rest = 64 - first
        out[pl.ds(first, 64), :] = mine[pl.ds(first, 64), :] + got[...]
        out[pl.ds(rest, 64), :] = mine[pl.ds(rest, 64), :]


def merge(others, spot, got, first):
    vmem = pl.BlockSpec(memory_space=VMEM)
    return pl.pallas_call(
        functools.partial(merge_kernel, first=first),
        out_shape=jax.ShapeDtypeStruct((128, RB), jnp.float32),
        grid=(1,),
        in_specs=[pl.BlockSpec((128, RB), lambda i: (spot, 0)), vmem],
        out_specs=vmem,
        compiler_params=pltpu.CompilerParams(vmem_limit_bytes=4 << 20),
        cost_estimate=pl.CostEstimate(flops=0, bytes_accessed=1 << 20, transcendentals=0),
        name="merge",
    )(others, got)


def finish_kernel(mine, ahead, behind, row, col, out):
    total = mine[...] + ahead[...] + behind[...]
    out[...] = (total / -(row[...] + col[...])).T.astype(jnp.bfloat16)


def finish(*parts):
    vmem = pl.BlockSpec(memory_space=VMEM)
    return pl.pallas_call(
        finish_kernel,
        out_shape=jax.ShapeDtypeStruct((RB, 128), jnp.bfloat16),
        grid=(1,),
        in_specs=[pl.BlockSpec((128, RB), lambda i: (6, 0))] + [vmem] * 4,
        out_specs=vmem,
        compiler_params=pltpu.CompilerParams(vmem_limit_bytes=8 << 20),
        name="finish",
    )(*parts)


def local(amplitudes, integrals, amp_mask, int_mask, occ_row, occ_col, vir_energy):
    y, x, z, core = (lax.axis_index(name) for name in AXES)
    place = jnp.stack([y, x, z]).astype(jnp.int32)
    own, oth, near, up, down, over = prepare(amp_mask, int_mask, amplitudes, integrals)

    from_down = send(up, UP)
    from_up = send(down, DOWN)
    from_over = send(over, OVER)
    from_near = send(near, CROSS)
    p0 = send(own, PARTNER)
    x0 = send(follow(oth, p0), ACROSS)

    own_rest, oth_rest, b_here, early = gather(
        near, from_near, from_down, from_up, from_over, own, p0, x0
    )
    b_down = send(b_here, UP)
    b_up = send(b_here, DOWN)
    p1 = send(own_rest, PARTNER)
    c1 = send(oth_rest, CROSS)
    x1 = send(oth_rest, ACROSS)
    b_far0 = send(b_down[:128], UP)
    b_far1 = send(b_up[128:], DOWN)
    slabs = join(place, b_here, b_down, b_up, b_far0, b_far1)

    amps = (early, own_rest, p1, c1, x1)
    keep_half = jnp.bitwise_xor(x // 2, core).astype(jnp.int32)
    give = arrange(place, (1 - keep_half)[None], amps)
    first_taken = send(jnp.dot(slabs[:128], give, preferred_element_type=jnp.float32), SWAP)
    taken = send(jnp.dot(slabs[128:], give, preferred_element_type=jnp.float32), SWAP)
    keep = arrange(place, keep_half[None], amps)

    farthest = jnp.dot(slabs[:128], keep, preferred_element_type=jnp.float32) + first_taken
    others = jnp.dot(slabs[128:], keep, preferred_element_type=jnp.float32) + taken
    ahead, behind = farthest[:64], farthest[64:]
    for step in range(3):
        ahead, behind = send(ahead, AHEAD), send(behind, BEHIND)
        ahead = merge(others, 2 * step, ahead, 0)
        behind = merge(others, 1 + 2 * step, behind, 64)
    ahead, behind = send(ahead, AHEAD), send(behind, BEHIND)

    row_x = jnp.where(core == 0, x, 3 - x)
    row_occ = lax.dynamic_slice(occ_row, (4 * row_x,), (4,))
    row_vir = lax.dynamic_slice(vir_energy, (y, 0), (1, 128))
    row_energy = (row_vir - row_occ[:, None]).reshape(1, RB)
    col_y, col_x = slab_of(x, z)
    col_occ = lax.dynamic_slice(occ_col, (col_x,), (1,))
    col_energy = (lax.dynamic_slice(vir_energy, (col_y, 0), (1, 128)) - col_occ).reshape(128, 1)
    return send(finish(others, ahead, behind, row_energy, col_energy), HOME)


def solution(mesh):
    grid = Mesh(mesh.devices.reshape(NY, NX, NZ, NC), AXES)
    layout, rep = ("y", "x"), ("z", "core")
    placed = (P(rep, layout, None), P(rep, None, layout), P(), P(), P(), P(), P())
    return jax.shard_map(
        local, mesh=grid, in_specs=placed, out_specs=P(layout, rep), check_vma=False
    )
```

```python
import functools

import jax
import jax.numpy as jnp
from jax import lax
from jax.experimental import pallas as pl
from jax.experimental.pallas import tpu as pltpu
from jax.sharding import Mesh, PartitionSpec as P

AXES = ("y", "x", "z", "core")
NY, NX, NZ, NC = 4, 4, 8, 2
KD = 192
RB = 512
KT = 16 * KD
VMEM = pltpu.MemorySpace.VMEM


def pairs(to):
    out = []
    for y in range(NY):
        for x in range(NX):
            for z in range(NZ):
                for c in range(NC):
                    ty, tx, tz, tc = to(y, x, z, c)
                    src = ((y * NX + x) * NZ + z) * NC + c
                    dst = ((ty % NY * NX + tx % NX) * NZ + tz % NZ) * NC + tc % NC
                    out.append((src, dst))
    return out


UP = pairs(lambda y, x, z, c: (y + 1, x, z, c))
DOWN = pairs(lambda y, x, z, c: (y - 1, x, z, c))
OVER = pairs(lambda y, x, z, c: (y + 2, x, z, c))
PARTNER = pairs(lambda y, x, z, c: (y, 3 - x, z, c))
CROSS = pairs(lambda y, x, z, c: (y, x ^ 1, z, c))
ACROSS = pairs(lambda y, x, z, c: (y, x + 2, z, c))
AHEAD = pairs(lambda y, x, z, c: (y, x, z + 1, c))
BEHIND = pairs(lambda y, x, z, c: (y, x, z - 1, c))
SWAP = pairs(lambda y, x, z, c: (y, x, z, 1 - c))


def slab_of(x, z):
    return z // 2, 2 * (x // 2) + z % 2


def home(y, x, z, c):
    col_y, col_x = slab_of(x, z)
    return y, x if c == 0 else 3 - x, 2 * col_y + col_x // 2, col_x % 2


HOME = pairs(home)


def send(value, where):
    return lax.ppermute(value, AXES, where)


def prepare_kernel(
    amp_mask, int_mask, a_any, b_any, own, oth, near, up, down, over, a, b, scratch, sems
):
    y, x = lax.axis_index("y"), lax.axis_index("x")
    block_q = 2 * y + x // 2
    low = jnp.minimum(x, 3 - x)
    turns = (y, lax.rem(y + 1, 4), lax.rem(y + 3, 4), lax.rem(y + 2, 4))
    moves = [pltpu.make_async_copy(b_any, b, sems.at[4])]
    for j, to_y in enumerate(turns):
        lanes = pl.ds(pl.multiple_of(to_y * 4 * RB, 4 * RB), 4 * RB)
        moves.append(pltpu.make_async_copy(a_any.at[:, :, lanes], a.at[j], sems.at[j]))
    for move in moves:
        move.start()
    moves[0].wait()
    for slab in range(16):
        keep = int_mask[y, slab // 2].astype(jnp.float32).astype(jnp.bfloat16)
        at = ((slab % 4) * 4 + slab // 4) * KD
        for k in range(3):
            scratch[pl.ds(at + k * 64, 64), :] = b[k, pl.ds(slab * 64, 64), :] * keep
    for j in range(KT // 128):
        near[pl.ds(0, 128), pl.ds(j * 128, 128)] = scratch[pl.ds(j * 128, 128), :].T
    for j, (first, second) in enumerate(
        ((own, oth), (up.at[0], up.at[1]), (down.at[0], down.at[1]), (over.at[0], over.at[1]))
    ):
        moves[1 + j].wait()
        keep = amp_mask[turns[j], block_q].astype(jnp.float32).astype(jnp.bfloat16)
        for dst, lo in ((first, low), (second, 1 - low)):
            for half in range(2):
                to_x = lo if half == 0 else 3 - lo
                start = pl.multiple_of(to_x * RB, RB)
                for k in range(3):
                    value = a[j, k, :, pl.ds(start, RB)] * keep
                    dst[pl.ds(k * 64, 64), pl.ds(half * RB, RB)] = value
                    if dst is oth:
                        near[pl.ds(128, 64), pl.ds((2 * k + half) * RB, RB)] = value


def prepare(amp_mask, int_mask, a, b):
    piece = jax.ShapeDtypeStruct((KD, 2 * RB), jnp.bfloat16)
    two = jax.ShapeDtypeStruct((2, KD, 2 * RB), jnp.bfloat16)
    near = jax.ShapeDtypeStruct((KD, KT), jnp.bfloat16)
    anywhere = pl.BlockSpec(memory_space=pl.ANY)
    vmem = pl.BlockSpec(memory_space=VMEM)
    return pl.pallas_call(
        prepare_kernel,
        out_shape=(piece, piece, near, two, two, two),
        grid_spec=pltpu.PrefetchScalarGridSpec(
            num_scalar_prefetch=2,
            grid=(1,),
            in_specs=[anywhere, anywhere],
            out_specs=(vmem,) * 6,
            scratch_shapes=[
                pltpu.VMEM((4, 3, 64, 4 * RB), jnp.bfloat16),
                pltpu.VMEM((3, 1024, 128), jnp.bfloat16),
                pltpu.VMEM((KT, 128), jnp.bfloat16),
                pltpu.SemaphoreType.DMA((5,)),
            ],
        ),
        compiler_params=pltpu.CompilerParams(vmem_limit_bytes=55 << 20),
        cost_estimate=pl.CostEstimate(flops=0, bytes_accessed=8 << 20, transcendentals=0),
        name="prepare",
    )(amp_mask, int_mask.T, a, b)


def follow_kernel(value, after, out):
    del after
    out[...] = value[...]


def follow(value, after):
    vmem = pl.BlockSpec(memory_space=VMEM)
    return pl.pallas_call(
        follow_kernel,
        out_shape=jax.ShapeDtypeStruct(value.shape, value.dtype),
        in_specs=[vmem, pl.BlockSpec(memory_space=pl.ANY)],
        out_specs=vmem,
        compiler_params=pltpu.CompilerParams(vmem_limit_bytes=4 << 20),
        cost_estimate=pl.CostEstimate(flops=0, bytes_accessed=1 << 20, transcendentals=0),
        name="follow",
    )(value, after)


def gather_kernel(
    near, from_near, down, up, over, own, p0, x0, own_rest, oth_rest, b_here, early
):
    for j, ref in enumerate((down, up, over)):
        own_rest[j] = ref[0]
        oth_rest[j] = ref[1]
    b_here[pl.ds(0, 128), :] = near[...]
    b_here[pl.ds(128, 128), :] = from_near[pl.ds(0, 128), :]
    for j, ref in ((0, own), (1, p0), (3, x0)):
        early[j] = ref[...]
    for k in range(3):
        early[2, pl.ds(k * 64, 64), :] = from_near[pl.ds(128, 64), pl.ds(k * 2 * RB, 2 * RB)]


def gather(*parts):
    def stack(n):
        return jax.ShapeDtypeStruct((n, KD, 2 * RB), jnp.bfloat16)

    vmem = pl.BlockSpec(memory_space=VMEM)
    return pl.pallas_call(
        gather_kernel,
        out_shape=(stack(3), stack(3), jax.ShapeDtypeStruct((256, KT), jnp.bfloat16), stack(4)),
        grid=(1,),
        in_specs=[pl.BlockSpec((128, KT), lambda i: (0, 0))] + [vmem] * 7,
        out_specs=(vmem,) * 4,
        compiler_params=pltpu.CompilerParams(vmem_limit_bytes=20 << 20),
        cost_estimate=pl.CostEstimate(flops=0, bytes_accessed=10 << 20, transcendentals=0),
        name="gather",
    )(*parts)


def run(moves, sems):
    copies = [pltpu.make_async_copy(src, dst, sems.at[i]) for i, (src, dst) in enumerate(moves)]
    for copy in copies:
        copy.start()
    for copy in copies:
        copy.wait()


def join_kernel(place, here, down, up, far0, far1, out, sems):
    y, odd, z = place[0], lax.rem(place[1], 2), place[2]
    moves = []
    for turn, first, second in ((0, here, here), (3, down, down), (1, up, up), (2, far0, far1)):
        at = lax.rem(y + turn, 4) * 2
        skip = 0 if first is far0 else 128
        for bit, src in ((odd, first.at[pl.ds(0, 128), :]), (1 - odd, second.at[pl.ds(skip, 128), :])):
            ahead = lax.rem(at + bit - z + 8, 8)
            spot = jnp.where(ahead == 0, 7, jnp.where(ahead < 5, 7 - 2 * ahead, 2 * ahead - 8))
            spot = jnp.maximum(spot, 0)
            moves.append((src, out.at[pl.ds(pl.multiple_of(spot * 128, 128), 128), :]))
    run(moves, sems)


def tails_kernel(down, up, far0, far1):
    far0[...] = down[...]
    far1[...] = up[...]


def tails(down, up):
    slab = jax.ShapeDtypeStruct((128, KT), jnp.bfloat16)
    top = pl.BlockSpec((128, KT), lambda i: (0, 0))
    return pl.pallas_call(
        tails_kernel,
        out_shape=(slab, slab),
        grid=(1,),
        in_specs=[top, pl.BlockSpec((128, KT), lambda i: (1, 0))],
        out_specs=(top, top),
        compiler_params=pltpu.CompilerParams(vmem_limit_bytes=10 << 20),
        cost_estimate=pl.CostEstimate(flops=0, bytes_accessed=3 << 20, transcendentals=0),
        name="tails",
    )(down, up)


def join(place, *parts):
    return pl.pallas_call(
        join_kernel,
        out_shape=jax.ShapeDtypeStruct((1024, KT), jnp.bfloat16),
        grid_spec=pltpu.PrefetchScalarGridSpec(
            num_scalar_prefetch=1,
            grid=(1,),
            in_specs=[pl.BlockSpec(memory_space=pl.ANY)] * 5,
            out_specs=pl.BlockSpec(memory_space=VMEM),
            scratch_shapes=[pltpu.SemaphoreType.DMA((8,))],
        ),
        compiler_params=pltpu.CompilerParams(vmem_limit_bytes=16 << 20),
        cost_estimate=pl.CostEstimate(flops=0, bytes_accessed=6 << 20, transcendentals=0),
        name="join",
    )(place, *parts)


def arrange_kernel(place, half, early, own_rest, p1, c1, x1, out, sems):
    y, x = place[0], place[1]
    lanes = pl.ds(pl.multiple_of(half[0] * RB, RB), RB)
    around = (lax.rem(y + 3, 4), lax.rem(y + 1, 4), lax.rem(y + 2, 4))
    sources = (x, 3 - x, x + 1 - 2 * lax.rem(x, 2), lax.rem(x + 2, 4))
    moves = []
    for j, (rest, from_x) in enumerate(zip((own_rest, p1, c1, x1), sources)):
        for ref, from_y in ((early.at[j], y), *((rest.at[i], at) for i, at in enumerate(around))):
            at = pl.multiple_of((from_x * 4 + from_y) * KD, KD)
            moves.append((ref.at[:, lanes], out.at[pl.ds(at, KD), :]))
    run(moves, sems)


def arrange(place, half, amps):
    return pl.pallas_call(
        arrange_kernel,
        out_shape=jax.ShapeDtypeStruct((KT, RB), jnp.bfloat16),
        grid_spec=pltpu.PrefetchScalarGridSpec(
            num_scalar_prefetch=2,
            grid=(1,),
            in_specs=[pl.BlockSpec(memory_space=pl.ANY)] * 5,
            out_specs=pl.BlockSpec(memory_space=VMEM),
            scratch_shapes=[pltpu.SemaphoreType.DMA((16,))],
        ),
        compiler_params=pltpu.CompilerParams(vmem_limit_bytes=16 << 20),
        cost_estimate=pl.CostEstimate(flops=0, bytes_accessed=6 << 20, transcendentals=0),
        name="arrange",
    )(place, half, *amps)


def merge_kernel(mine, got, out, *, first):
    if got.shape[0] == mine.shape[0]:
        out[...] = mine[...] + got[...]
    else:
        rest = 64 - first
        out[pl.ds(first, 64), :] = mine[pl.ds(first, 64), :] + got[...]
        out[pl.ds(rest, 64), :] = mine[pl.ds(rest, 64), :]


def merge(others, spot, got, first):
    vmem = pl.BlockSpec(memory_space=VMEM)
    return pl.pallas_call(
        functools.partial(merge_kernel, first=first),
        out_shape=jax.ShapeDtypeStruct((128, RB), jnp.float32),
        grid=(1,),
        in_specs=[pl.BlockSpec((128, RB), lambda i: (spot, 0)), vmem],
        out_specs=vmem,
        compiler_params=pltpu.CompilerParams(vmem_limit_bytes=4 << 20),
        cost_estimate=pl.CostEstimate(flops=0, bytes_accessed=1 << 20, transcendentals=0),
        name="merge",
    )(others, got)


def finish_kernel(mine, ahead, behind, row, col, out):
    total = mine[...] + ahead[...] + behind[...]
    out[...] = (total / -(row[...] + col[...])).T.astype(jnp.bfloat16)


def finish(*parts):
    vmem = pl.BlockSpec(memory_space=VMEM)
    return pl.pallas_call(
        finish_kernel,
        out_shape=jax.ShapeDtypeStruct((RB, 128), jnp.bfloat16),
        grid=(1,),
        in_specs=[pl.BlockSpec((128, RB), lambda i: (6, 0))] + [vmem] * 4,
        out_specs=vmem,
        compiler_params=pltpu.CompilerParams(vmem_limit_bytes=8 << 20),
        name="finish",
    )(*parts)


def local(amplitudes, integrals, amp_mask, int_mask, occ_row, occ_col, vir_energy):
    y, x, z, core = (lax.axis_index(name) for name in AXES)
    place = jnp.stack([y, x, z]).astype(jnp.int32)
    own, oth, near, up, down, over = prepare(amp_mask, int_mask, amplitudes, integrals)

    from_down = send(up, UP)
    from_up = send(down, DOWN)
    from_over = send(over, OVER)
    from_near = send(near, CROSS)
    p0 = send(own, PARTNER)
    x0 = send(follow(oth, p0), ACROSS)

    own_rest, oth_rest, b_here, early = gather(
        near, from_near, from_down, from_up, from_over, own, p0, x0
    )
    b_down = send(b_here, UP)
    b_up = send(b_here, DOWN)
    p1 = send(own_rest, PARTNER)
    c1 = send(oth_rest, CROSS)
    x1 = send(oth_rest, ACROSS)
    far0, far1 = tails(b_down, b_up)
    b_far0 = send(far0, UP)
    b_far1 = send(far1, DOWN)
    slabs = join(place, b_here, b_down, b_up, b_far0, b_far1)

    amps = (early, own_rest, p1, c1, x1)
    keep_half = jnp.bitwise_xor(x // 2, core).astype(jnp.int32)
    give = arrange(place, (1 - keep_half)[None], amps)
    first_taken = send(jnp.dot(slabs[:128], give, preferred_element_type=jnp.float32), SWAP)
    taken = send(jnp.dot(slabs[128:], give, preferred_element_type=jnp.float32), SWAP)
    keep = arrange(place, keep_half[None], amps)

    farthest = jnp.dot(slabs[:128], keep, preferred_element_type=jnp.float32) + first_taken
    others = jnp.dot(slabs[128:], keep, preferred_element_type=jnp.float32) + taken
    ahead, behind = farthest[:64], farthest[64:]
    for step in range(3):
        ahead, behind = send(ahead, AHEAD), send(behind, BEHIND)
        ahead = merge(others, 2 * step, ahead, 0)
        behind = merge(others, 1 + 2 * step, behind, 64)
    ahead, behind = send(ahead, AHEAD), send(behind, BEHIND)

    row_x = jnp.where(core == 0, x, 3 - x)
    row_occ = lax.dynamic_slice(occ_row, (4 * row_x,), (4,))
    row_vir = lax.dynamic_slice(vir_energy, (y, 0), (1, 128))
    row_energy = (row_vir - row_occ[:, None]).reshape(1, RB)
    col_y, col_x = slab_of(x, z)
    col_occ = lax.dynamic_slice(occ_col, (col_x,), (1,))
    col_energy = (lax.dynamic_slice(vir_energy, (col_y, 0), (1, 128)) - col_occ).reshape(128, 1)
    return send(finish(others, ahead, behind, row_energy, col_energy), HOME)


def solution(mesh):
    grid = Mesh(mesh.devices.reshape(NY, NX, NZ, NC), AXES)
    layout, rep = ("y", "x"), ("z", "core")
    placed = (P(rep, layout, None), P(rep, None, layout), P(), P(), P(), P(), P())
    return jax.shard_map(
        local, mesh=grid, in_specs=placed, out_specs=P(layout, rep), check_vma=False
    )
```
